512 devices in a mesh: blk: 64 (over y, x, z_lo), group: 8 (over z_hi, core).
Axes of the slice: x: 4, y: 8, z: 8 (z_hi: 4, z_lo: 2; z = z_hi * 2 + z_lo), core: 2. Of those that a mesh axis runs over, the one named last changes fastest.
Arguments:
- tokens: bfloat16 [8, 32768, 1024], P('group', 'blk'), may hold values from -6 to 6
- norm_gain: float32 [1024], replicated, may hold values from 0.5 to 2
- proj_weight: bfloat16 [1024, 1024], replicated, may hold values from -0.1875 to 0.1875
- text_feats: bfloat16 [8, 2048, 1024], P('group', 'blk'), may hold values from -6 to 6
- lengths: int32 [8, 64, 32], P('group', 'blk'), may hold values from 1 to 48, 512 in all within a row
- positives: int32 [8, 2048], P('group', 'blk'), may hold values from 0 to 2047, each once within a row
- sample_weight: float32 [8, 2048], P('group', 'blk'), may hold values from 0.5 to 13.5
- log_temp: float32 [], replicated, may hold values from 3.9 to 4.6
- logit_bias: float32 [], replicated, may hold values from -11 to -7
- loss_scale: float32 [], replicated, may hold values from 4194304 to 16777216
Outputs:
- grad_tokens: bfloat16 [8, 32768, 1024], P('group', 'blk')
- grad_texts: float32 [8, 2048, 1024], P('group', 'blk')
- loss_value: float32 [], replicated
- grad_temp: float32 [], replicated
- grad_bias: float32 [], replicated
The draws below stay inside these ranges and needn't reach their ends.
Inputs may be any that keep to these rules, and one draw needn't show every extreme that they name: The 32 lengths of one device sum to 512, and that device's tokens hold its sketches one after another in order. In each cycle a permutation: sketch i of the cycle is paired with text positives[i] of the cycle.
All inputs are finite; a program needn't handle non-finite values.
Results may differ from the reference program's by a relative error of at most 0.023.
Values may be sent and summed in bfloat16 or wider, within the bound.
No kernel may reach another device: no remote copies, remote signals or barrier semaphores. Data moves between devices by JAX's collectives and lax.ppermute only.
A program may use at most 64 MiB of HBM per device.

```python
import math
import jax
import jax.numpy as jnp
import numpy as np
from jax import lax

D = 1024
E = 1024
SKETCH_DEV = 32
MAXLEN = 48
TOK_DEV = 512
CYCLE_DEVS = 64
CYCLES = 8
CYCLE_B = 2048
TOK_CYCLE = 32768


def draw_sample_weight(key, part):
    key = jax.random.fold_in(key, 11)
    place = jnp.arange(CYCLE_B, dtype=jnp.float32) / CYCLE_B
    rough = jax.random.uniform(key, (CYCLES, CYCLE_B), jnp.float32, 0.7, 1.3)
    return jnp.exp(jnp.log(3.0) * place)[None, :] * rough


def steps_of(own_key, shape, shards, low, top_value):
    def one(dim, blocks):
        steps = jax.random.uniform(jax.random.fold_in(jax.random.fold_in(own_key, 6), dim), (blocks,), jnp.float32, low / len(shards), top_value / len(shards))
        return jnp.repeat(jnp.exp(steps), shape[dim] // blocks).reshape((-1,) + (1,) * (len(shape) - dim - 1))

    loudness = one(*shards[0])
    for cut in shards[1:]:
        loudness = loudness * one(*cut)
    return loudness


def length_profile(count, total, reach, skew):
    weights = [(1 << 20) // math.isqrt(grade ** skew) + 1 for grade in range(2, count + 1)]
    spare, given = total - reach - (count - 1), [1] * (count - 1)
    while spare > 0:
        candidates = [i for i in range(count - 1) if given[i] < reach]
        pool, budget = sum([weights[i] for i in candidates]), spare
        for i in candidates:
            addition = min(reach - given[i], max(1, budget * weights[i] // pool), spare)
            given[i] = given[i] + addition
            spare = spare - addition
    return np.array([reach] + given)


def uneven_parts(key, amount, total, bound, slope):
    if amount == 2:
        one = jax.random.randint(key, (), max(1, total - bound), min(bound, total - 1) + 1)
        return jnp.stack([one, total - one])
    tallies = jnp.asarray(length_profile(amount, total, bound, slope), jnp.int32)
    couples = (amount - 1) // 2
    source_of, receiver = tallies[1:1 + 2 * couples:2], tallies[2:2 + 2 * couples:2]
    slack = jnp.minimum(source_of - 1, bound - receiver)
    moved = jax.random.randint(jax.random.fold_in(key, 1), (couples,), 0, 1 << 20) % (slack + 1)
    tallies = tallies.at[1:1 + 2 * couples:2].set(source_of - moved).at[2:2 + 2 * couples:2].set(receiver + moved)
    return tallies[jax.random.permutation(jax.random.fold_in(key, 2), amount)]


def normal_values(rng, shape, width, most, cuts=(), kind=jnp.bfloat16):
    result = jax.random.normal(rng, shape, jnp.float32) * width
    if len(cuts) > 0:
        result = steps_of(rng, shape, cuts, -0.22, 0.18) * result
    return jnp.clip(result, min=-most, max=most).astype(kind)


def setup_inputs(seed: int = 0) -> dict:
    seeds = jax.random.split(jax.random.key(seed), 11)
    return {
        "tokens": normal_values(seeds[0], (CYCLES, TOK_CYCLE, D), 1.0, 6.0, ((0, 8), (1, 64))),
        "norm_gain": jnp.clip(jnp.exp(jax.random.uniform(seeds[1], (D,), jnp.float32, math.log(0.5), math.log(2.0))), 0.5, 2.0),
        "proj_weight": normal_values(seeds[2], (D, E), D ** -0.5, 0.1875),
        "text_feats": normal_values(seeds[3], (CYCLES, CYCLE_B, E), 1.0, 6.0, ((0, 8), (1, 64))),
        "lengths": jax.vmap(lambda own: uneven_parts(own, SKETCH_DEV, TOK_DEV, MAXLEN, 2))(jax.random.split(seeds[4], CYCLES * CYCLE_DEVS)).reshape((CYCLES, CYCLE_DEVS, SKETCH_DEV)).astype(jnp.int32),
        "positives": jax.vmap(lambda own: jax.random.permutation(own, CYCLE_B))(jax.random.split(seeds[5], CYCLES)).reshape((CYCLES, CYCLE_B)).astype(jnp.int32),
        "sample_weight": draw_sample_weight(jax.random.fold_in(seeds[10], 71), 0),
        "log_temp": jnp.clip(jax.random.uniform(seeds[7], (), jnp.float32, 3.9, 4.6), 3.9, 4.6),
        "logit_bias": jnp.clip(jax.random.uniform(seeds[8], (), jnp.float32, -11.0, -7.0), -11.0, -7.0),
        "loss_scale": jnp.clip(jnp.exp(jax.random.uniform(seeds[9], (), jnp.float32, math.log(4194304), math.log(16777216))), 4194304, 16777216),
    }


EPSILON = 1e-06
GELU_SCALE = 0.7978845608028654

def gelu_value(values):
    inner_arg = GELU_SCALE * (values + 0.044715 * values * values * values)
    return 0.5 * values * (1.0 + jnp.tanh(inner_arg))

def gelu_slope(values):
    inner_arg = GELU_SCALE * (values + 0.044715 * values * values * values)
    tanh_part = jnp.tanh(inner_arg)
    return 0.5 * (1.0 + tanh_part) + 0.5 * values * (1.0 - tanh_part * tanh_part) * GELU_SCALE * (1.0 + 3.0 * 0.044715 * values * values)

def reference(tokens, norm_gain, proj_weight, text_feats, lengths, positives, sample_weight, log_temp, logit_bias, loss_scale):
    temper = jnp.exp(log_temp)
    inv_count = 1.0 / (CYCLES * CYCLE_B)
    columns = jnp.arange(CYCLE_B, dtype=jnp.int32)

    def one_cycle(operands):
        tok_cycle, txt_cycle, len_cycle, pos_cycle, wgt_cycle = operands
        inputs = tok_cycle.astype(jnp.float32)
        inv_rms = lax.rsqrt(lax.optimization_barrier(jnp.mean(inputs * inputs, axis=-1, keepdims=True)) + EPSILON)
        normal_x = inputs * inv_rms
        normed = (normal_x * norm_gain).astype(jnp.bfloat16)
        preact = jnp.dot(normed, proj_weight, preferred_element_type=jnp.float32)
        activated = gelu_value(preact).astype(jnp.bfloat16)
        seg_ends = jnp.cumsum(len_cycle, axis=-1).astype(jnp.int32)
        local_pos = jnp.arange(TOK_DEV, dtype=jnp.int32)
        seg_local = lax.optimization_barrier(jnp.sum((local_pos[None, :, None] >= seg_ends[:, None, :]).astype(jnp.int32), axis=-1))
        sketch_of = (seg_local + jnp.arange(CYCLE_DEVS, dtype=jnp.int32)[:, None] * SKETCH_DEV).reshape(-1).astype(jnp.int32)
        membership = (seg_local[:, None, :] == jnp.arange(SKETCH_DEV, dtype=jnp.int32)[None, :, None]).astype(jnp.float32)
        act_blocks = activated.astype(jnp.float32).reshape(CYCLE_DEVS, TOK_DEV, E)
        len_col = len_cycle.reshape(CYCLE_B, 1).astype(jnp.float32)
        pooled = jnp.einsum('nkt,nte->nke', membership, act_blocks, precision=lax.Precision.HIGHEST).reshape(CYCLE_B, E) / len_col
        pool_rnorm = lax.rsqrt(lax.optimization_barrier(jnp.sum(pooled * pooled, axis=-1, keepdims=True)) + EPSILON)
        sketch_unit = pooled * pool_rnorm
        sketch_embed = sketch_unit.astype(jnp.bfloat16)
        text_in = txt_cycle.astype(jnp.float32)
        text_rnorm = lax.rsqrt(lax.optimization_barrier(jnp.sum(text_in * text_in, axis=-1, keepdims=True)) + EPSILON)
        text_unit = text_in * text_rnorm
        text_embed = text_unit.astype(jnp.bfloat16)

        def row_block(cycle_carry, block_in):
            text_grad, loss_sum, temp_sum, bias_sum = cycle_carry
            rows_embed, rows_pos, rows_wgt = block_in
            dot_scores = lax.dot_general(rows_embed, text_embed, (((1,), (1,)), ((), ())), preferred_element_type=jnp.float32)
            logits = temper * dot_scores + logit_bias
            pair_signs = jnp.where(rows_pos[:, None] == columns[None, :], 1.0, -1.0).astype(jnp.float32)
            pair_loss = jax.nn.softplus(-pair_signs * logits)
            coeffs = -rows_wgt[:, None] * pair_signs * jax.nn.sigmoid(-pair_signs * logits) * inv_count
            scaled_coef = (coeffs * (temper * loss_scale)).astype(jnp.bfloat16)
            sketch_rows = jnp.dot(scaled_coef, text_embed, preferred_element_type=jnp.float32)
            text_grad = text_grad + lax.dot_general(scaled_coef, rows_embed, (((0,), (0,)), ((), ())), preferred_element_type=jnp.float32)
            loss_sum = loss_sum + jnp.sum(rows_wgt[:, None] * pair_loss) * inv_count
            temp_sum = temp_sum + jnp.sum(coeffs * temper * dot_scores)
            bias_sum = bias_sum + jnp.sum(coeffs)
            return ((text_grad, loss_sum, temp_sum, bias_sum), sketch_rows)
        start = (jnp.zeros((CYCLE_B, E), jnp.float32), jnp.zeros((), jnp.float32), jnp.zeros((), jnp.float32), jnp.zeros((), jnp.float32))
        blocks_in = (sketch_embed.reshape(CYCLE_DEVS, SKETCH_DEV, E), pos_cycle.reshape(CYCLE_DEVS, SKETCH_DEV), wgt_cycle.reshape(CYCLE_DEVS, SKETCH_DEV))
        (text_grad, loss_sum, temp_sum, bias_sum), sketch_grad = lax.scan(row_block, start, blocks_in)
        sketch_grad = sketch_grad.reshape(CYCLE_B, E)
        along_unit = lax.optimization_barrier(jnp.sum(sketch_unit * sketch_grad, axis=-1, keepdims=True))
        pool_grad = pool_rnorm * (sketch_grad - sketch_unit * along_unit)
        per_token = (pool_grad / len_col)[sketch_of]
        act_grad = (per_token * gelu_slope(preact)).astype(jnp.bfloat16)
        normed_grad = lax.dot_general(act_grad, proj_weight, (((1,), (1,)), ((), ())), preferred_element_type=jnp.float32)
        gain_part = normed_grad * norm_gain
        token_grad = inv_rms * (gain_part - normal_x * lax.optimization_barrier(jnp.mean(gain_part * normal_x, axis=-1, keepdims=True)))
        text_along = lax.optimization_barrier(jnp.sum(text_unit * text_grad, axis=-1, keepdims=True))
        text_out = text_rnorm * (text_grad - text_unit * text_along)
        return (token_grad.astype(jnp.bfloat16), text_out, loss_sum, temp_sum, bias_sum)
    grad_tokens, grad_texts, losses, temp_terms, bias_terms = lax.map(one_cycle, (tokens, text_feats, lengths, positives, sample_weight))
    return (grad_tokens, grad_texts, jnp.sum(losses), jnp.sum(temp_terms), jnp.sum(bias_terms))
```

```python
import functools

import jax
import jax.numpy as jnp
from jax import lax
from jax.experimental import pallas as pl
from jax.experimental.pallas import tpu as pltpu
from jax.sharding import PartitionSpec as P

EPSILON = 1e-06
GELU_SCALE = 0.7978845608028654
GELU_CUBE = 0.044715
LANES = 128
VMEM_LIMIT = 48 * 1024 * 1024
F32 = jnp.float32
BF16 = jnp.bfloat16

VMEM = pl.BlockSpec(memory_space=pltpu.VMEM)
SMEM = pl.BlockSpec(memory_space=pltpu.SMEM)


def params():
    return pltpu.CompilerParams(vmem_limit_bytes=VMEM_LIMIT)


def three_parts(values):
    high = values.astype(BF16).astype(F32)
    rest = values - high
    middle = rest.astype(BF16).astype(F32)
    return high, middle, rest - middle


def rows_to_column(row, count):
    here = lax.broadcasted_iota(jnp.int32, (count, count), 0)
    there = lax.broadcasted_iota(jnp.int32, (count, count), 1)
    return jnp.sum(jnp.where(here == there, row, 0.0), axis=1, keepdims=True)


def text_kernel(text_ref, out_ref):
    text_in = text_ref[0].astype(F32)
    text_rnorm = lax.rsqrt(jnp.sum(text_in * text_in, axis=-1, keepdims=True) + EPSILON)
    text_embed = (text_in * text_rnorm).astype(BF16)
    for member in range(out_ref.shape[0]):
        out_ref[member] = text_embed


def forward_kernel(
    tokens_ref,
    gain_ref,
    weight_ref,
    lengths_ref,
    positives_ref,
    sample_ref,
    send_ref,
    slope_ref,
    pooled_ref,
    normed_ref,
):
    step = pl.program_id(0)
    sketches = lengths_ref.shape[-1]
    tok_count = tokens_ref.shape[1]
    width = weight_ref.shape[1]

    @pl.when(step == 0)
    def _():
        inputs = tokens_ref[0].astype(F32)
        inv_rms = lax.rsqrt(jnp.mean(inputs * inputs, axis=-1, keepdims=True) + EPSILON)
        normed_ref[...] = (inputs * inv_rms * gain_ref[...]).astype(BF16)

    lens_row = lengths_ref[0].astype(F32)
    lens_col = rows_to_column(lens_row, sketches)
    here = lax.broadcasted_iota(jnp.int32, (sketches, sketches), 0)
    there = lax.broadcasted_iota(jnp.int32, (sketches, sketches), 1)
    ends = jnp.sum(jnp.where(there <= here, lens_row, 0.0), axis=1, keepdims=True)
    place = lax.broadcasted_iota(jnp.int32, (sketches, tok_count), 1).astype(F32)
    membership = jnp.where((place < ends) & (place >= ends - lens_col), 1.0, 0.0).astype(BF16)

    values = jnp.dot(normed_ref[...], weight_ref[...], preferred_element_type=F32)
    square = values * values
    tanh_part = jnp.tanh(values * (GELU_SCALE + (GELU_SCALE * GELU_CUBE) * square))
    half = 0.5 + 0.5 * tanh_part
    activated = (values * half).astype(BF16)
    slope = half + values * (1.0 - tanh_part * tanh_part) * (
        0.5 * GELU_SCALE + (1.5 * GELU_SCALE * GELU_CUBE) * square
    )
    slope_ref[...] = slope.astype(BF16)
    pooled = jnp.dot(membership, activated, preferred_element_type=F32) / lens_col
    pooled_ref[:, pl.ds(pl.multiple_of(step * width, width), width)] = pooled

    @pl.when(step == pl.num_programs(0) - 1)
    def _():
        all_pooled = pooled_ref[...]
        rnorm = lax.rsqrt(jnp.sum(all_pooled * all_pooled, axis=-1, keepdims=True) + EPSILON)
        embed = (all_pooled * rnorm).astype(BF16)
        paired = rows_to_column(positives_ref[...].astype(F32), sketches)
        paired_high = jnp.floor(paired * (1.0 / 16.0))
        weight = three_parts(rows_to_column(sample_ref[...], sketches))
        columns = (paired_high, paired - 16.0 * paired_high) + weight
        lane = lax.broadcasted_iota(jnp.int32, (sketches, LANES), 1)
        extra = jnp.zeros((sketches, LANES), F32)
        for i, column in enumerate(columns):
            extra = jnp.where(lane == i, column, extra)
        extra = extra.astype(BF16)
        features = embed.shape[1]
        for member in range(send_ref.shape[0]):
            send_ref[member, :, :features] = embed
            send_ref[member, :, features:] = extra


def score_kernel(inv_count, cols, blk_ref, log_temp_ref, bias_ref, scale_ref, sketch_ref, text_ref, out_s_ref, out_t_ref):
    members, sketches, features = text_ref.shape
    rows = members * sketches
    sketch = sketch_ref[:, :, :features].reshape(rows, features)
    text = text_ref[...].reshape(rows, features)
    extra = sketch_ref[:, :, features:].reshape(rows, LANES).astype(F32)
    paired = extra[:, 0:1] * 16.0 + extra[:, 1:2]
    weight = (extra[:, 2:3] + extra[:, 3:4]) + extra[:, 4:5]
    weight = weight * inv_count
    dots = lax.dot_general(sketch, text, (((1,), (1,)), ((), ())), preferred_element_type=F32)
    temper = jnp.exp(jnp.full((1, 1), log_temp_ref[0], F32))
    logits = temper * dots + bias_ref[0]
    column = lax.broadcasted_iota(jnp.int32, (1, rows), 1)
    column = (column // sketches) * (cols * sketches) + (blk_ref[0] % cols) * sketches + column % sketches
    is_pair = paired == column.astype(F32)
    signs = jnp.where(is_pair, 1.0, -1.0)
    against = jnp.where(is_pair, -logits, logits)
    decay = jnp.exp(-jnp.abs(against))
    chance = jnp.where(against >= 0.0, 1.0, decay) / (1.0 + decay)
    pair_loss = jnp.maximum(against, 0.0) + jnp.log1p(decay)
    coeffs = -weight * signs * chance
    scaled = (coeffs * (temper * scale_ref[0])).astype(BF16)
    sketch_part = jnp.dot(scaled, text, preferred_element_type=F32).astype(BF16)
    text_part = lax.dot_general(scaled, sketch, (((0,), (0,)), ((), ())), preferred_element_type=F32).astype(BF16)
    out_t_ref[...] = text_part.reshape(text_ref.shape)
    out_s_ref[:, :, :features] = sketch_part.reshape(text_ref.shape)

    def total(values):
        return jnp.sum(jnp.sum(values, axis=1, keepdims=True), axis=0, keepdims=True)

    lane = lax.broadcasted_iota(jnp.int32, (sketches, LANES), 1)
    sums = jnp.zeros((sketches, LANES), F32)
    for i, value in enumerate((total(weight * pair_loss), total(coeffs * temper * dots), total(coeffs))):
        for j, piece in enumerate(three_parts(value)):
            sums = jnp.where(lane == 3 * j + i, piece, sums)
    sums = sums.astype(BF16)
    for member in range(members):
        out_s_ref[member, :, features:] = sums


def first_sums_kernel(in_ref, out_ref):
    members = in_ref.shape[0]
    gathered = jnp.zeros((8, LANES), F32)
    for member in range(members):
        gathered = gathered + in_ref[member, :8, :].astype(F32)
    lane = lax.broadcasted_iota(jnp.int32, (8, LANES), 1)
    result = jnp.zeros((8, LANES), F32)
    for i in range(3):
        value = gathered[:, i : i + 1] + (gathered[:, i + 3 : i + 4] + gathered[:, i + 6 : i + 7])
        result = jnp.where(lane == i, value, result)
    for member in range(out_ref.shape[0]):
        out_ref[member] = result


def next_sums_kernel(in_ref, out_ref):
    result = jnp.sum(in_ref[...], axis=0)
    for member in range(out_ref.shape[0]):
        out_ref[member] = result


def last_sums_kernel(in_ref, loss_ref, temp_ref, bias_ref):
    result = jnp.sum(in_ref[...], axis=0)
    loss_ref[...] = result[0:1, 0:1]
    temp_ref[...] = result[0:1, 1:2]
    bias_ref[...] = result[0:1, 2:3]


def backward_kernel(parts_ref, pooled_ref, lengths_ref, slope_ref, tokens_ref, gain_ref, weight_ref, out_ref, grad_ref):
    step = pl.program_id(0)
    sketches = lengths_ref.shape[-1]
    block = slope_ref.shape[0]
    lens_row = lengths_ref[0].astype(F32)
    lens_col = rows_to_column(lens_row, sketches)

    @pl.when(step == 0)
    def _():
        sketch_grad = jnp.sum(parts_ref[...].astype(F32), axis=0)
        pooled = pooled_ref[...]
        rnorm = lax.rsqrt(jnp.sum(pooled * pooled, axis=-1, keepdims=True) + EPSILON)
        unit = pooled * rnorm
        along = jnp.sum(unit * sketch_grad, axis=-1, keepdims=True)
        pool_grad = rnorm * (sketch_grad - unit * along) / lens_col
        high = pool_grad.astype(BF16)
        grad_ref[:sketches] = high
        grad_ref[sketches:] = (pool_grad - high.astype(F32)).astype(BF16)

    here = lax.broadcasted_iota(jnp.int32, (sketches, sketches), 0)
    there = lax.broadcasted_iota(jnp.int32, (sketches, sketches), 1)
    ends = jnp.sum(jnp.where(here <= there, lens_col, 0.0), axis=0, keepdims=True)
    place = lax.broadcasted_iota(jnp.int32, (block, sketches), 0).astype(F32) + (step * block).astype(F32)
    membership = jnp.where((place < ends) & (place >= ends - lens_row), 1.0, 0.0).astype(BF16)
    per_token = jnp.dot(membership, grad_ref[:sketches], preferred_element_type=F32) + jnp.dot(
        membership, grad_ref[sketches:], preferred_element_type=F32
    )
    act_grad = (per_token * slope_ref[...].astype(F32)).astype(BF16)
    normed_grad = lax.dot_general(
        act_grad, weight_ref[...], (((1,), (1,)), ((), ())), preferred_element_type=F32
    )
    inputs = tokens_ref[0].astype(F32)
    inv_rms = lax.rsqrt(jnp.mean(inputs * inputs, axis=-1, keepdims=True) + EPSILON)
    normal_x = inputs * inv_rms
    gain_part = normed_grad * gain_ref[...]
    token_grad = inv_rms * (gain_part - normal_x * jnp.mean(gain_part * normal_x, axis=-1, keepdims=True))
    out_ref[0] = token_grad.astype(BF16)


def text_grad_kernel(parts_ref, text_ref, out_ref):
    text_grad = jnp.sum(parts_ref[...].astype(F32), axis=0)
    text_in = text_ref[0].astype(F32)
    rnorm = lax.rsqrt(jnp.sum(text_in * text_in, axis=-1, keepdims=True) + EPSILON)
    unit = text_in * rnorm
    along = jnp.sum(unit * text_grad, axis=-1, keepdims=True)
    out_ref[0] = rnorm * (text_grad - unit * along)


def on_device(cycle_size, cycles, tokens, norm_gain, proj_weight, text_feats, lengths, positives, sample_weight, log_temp, logit_bias, loss_scale):
    tok_count, depth = tokens.shape[1:]
    features = proj_weight.shape[1]
    sketches = text_feats.shape[1]
    members = 8
    cols = cycle_size // members
    row_groups = [[r * members + c for c in range(members)] for r in range(cols)]
    col_groups = [[r * members + c for r in range(cols)] for c in range(members)]
    inv_count = 1.0 / (cycles * cycle_size * sketches)
    wide = features + LANES
    gain = norm_gain.reshape(1, depth)
    lens = lengths.reshape(1, 1, sketches)

    def exchange(values, groups):
        return lax.all_to_all(values, "blk", 0, 0, axis_index_groups=groups, tiled=True)

    text_send = pl.pallas_call(
        text_kernel,
        out_shape=jax.ShapeDtypeStruct((cols, sketches, features), BF16),
        in_specs=[VMEM],
        out_specs=VMEM,
        name="text_embed",
    )(text_feats)
    text_all = exchange(text_send, col_groups)

    steps = 4
    width = features // steps
    sketch_send, slope, pooled = pl.pallas_call(
        forward_kernel,
        grid=(steps,),
        out_shape=(
            jax.ShapeDtypeStruct((members, sketches, wide), BF16),
            jax.ShapeDtypeStruct((tok_count, features), BF16),
            jax.ShapeDtypeStruct((sketches, features), F32),
        ),
        in_specs=[
            pl.BlockSpec((1, tok_count, depth), lambda i: (0, 0, 0)),
            pl.BlockSpec((1, depth), lambda i: (0, 0)),
            pl.BlockSpec((depth, width), lambda i: (0, i)),
            pl.BlockSpec((1, 1, sketches), lambda i: (0, 0, 0)),
            pl.BlockSpec((1, sketches), lambda i: (0, 0)),
            pl.BlockSpec((1, sketches), lambda i: (0, 0)),
        ],
        out_specs=(
            pl.BlockSpec((members, sketches, wide), lambda i: (0, 0, 0)),
            pl.BlockSpec((tok_count, width), lambda i: (0, i)),
            pl.BlockSpec((sketches, features), lambda i: (0, 0)),
        ),
        scratch_shapes=[pltpu.VMEM((tok_count, depth), BF16)],
        compiler_params=params(),
        cost_estimate=pl.CostEstimate(flops=2 * tok_count * depth * features, bytes_accessed=5 << 20, transcendentals=tok_count * features),
        name="forward",
    )(tokens, gain, proj_weight, lens, positives, sample_weight)
    sketch_all = exchange(sketch_send, row_groups)

    blk = lax.axis_index("blk").astype(jnp.int32).reshape(1)
    sketch_parts, text_parts = pl.pallas_call(
        functools.partial(score_kernel, inv_count, members),
        out_shape=(
            jax.ShapeDtypeStruct((members, sketches, wide), BF16),
            jax.ShapeDtypeStruct((cols, sketches, features), BF16),
        ),
        in_specs=[SMEM, SMEM, SMEM, SMEM, VMEM, VMEM],
        out_specs=(VMEM, VMEM),
        compiler_params=params(),
        name="score",
    )(blk, log_temp.reshape(1), logit_bias.reshape(1), loss_scale.reshape(1), sketch_all, text_all)
    sketch_back = exchange(sketch_parts, row_groups)
    text_back = exchange(text_parts, col_groups)

    row_sums = pl.pallas_call(
        first_sums_kernel,
        grid=(1,),
        out_shape=jax.ShapeDtypeStruct((cols, 8, LANES), F32),
        in_specs=[pl.BlockSpec((members, sketches, LANES), lambda i: (0, 0, features // LANES))],
        out_specs=pl.BlockSpec((cols, 8, LANES), lambda i: (0, 0, 0)),
        name="row_sums",
    )(sketch_back)
    cycle_parts = exchange(row_sums, col_groups)
    cycle_sums = pl.pallas_call(
        next_sums_kernel,
        out_shape=jax.ShapeDtypeStruct((cycles, 8, LANES), F32),
        in_specs=[VMEM],
        out_specs=VMEM,
        name="cycle_sums",
    )(cycle_parts)
    all_parts = lax.all_to_all(cycle_sums, "group", 0, 0, tiled=True)
    scalar = jax.ShapeDtypeStruct((1, 1), F32)
    loss_value, grad_temp, grad_bias = pl.pallas_call(
        last_sums_kernel,
        out_shape=(scalar, scalar, scalar),
        in_specs=[VMEM],
        out_specs=(VMEM, VMEM, VMEM),
        name="all_sums",
    )(all_parts)

    block = 128
    grad_tokens = pl.pallas_call(
        backward_kernel,
        grid=(tok_count // block,),
        out_shape=jax.ShapeDtypeStruct(tokens.shape, BF16),
        in_specs=[
            pl.BlockSpec((members, sketches, features), lambda i: (0, 0, 0)),
            pl.BlockSpec((sketches, features), lambda i: (0, 0)),
            pl.BlockSpec((1, 1, sketches), lambda i: (0, 0, 0)),
            pl.BlockSpec((block, features), lambda i: (i, 0)),
            pl.BlockSpec((1, block, depth), lambda i: (0, i, 0)),
            pl.BlockSpec((1, depth), lambda i: (0, 0)),
            pl.BlockSpec((depth, features), lambda i: (0, 0)),
        ],
        out_specs=pl.BlockSpec((1, block, depth), lambda i: (0, i, 0)),
        scratch_shapes=[pltpu.VMEM((2 * sketches, features), BF16)],
        compiler_params=params(),
        cost_estimate=pl.CostEstimate(flops=2 * tok_count * depth * features, bytes_accessed=5 << 20, transcendentals=0),
        name="backward",
    )(sketch_back, pooled, lens, slope, tokens, gain, proj_weight)

    grad_texts = pl.pallas_call(
        text_grad_kernel,
        out_shape=jax.ShapeDtypeStruct(text_feats.shape, F32),
        in_specs=[VMEM, VMEM],
        out_specs=VMEM,
        name="text_grad",
    )(text_back, text_feats)
    return (grad_tokens, grad_texts, loss_value.reshape(()), grad_temp.reshape(()), grad_bias.reshape(()))


def solution(mesh):
    placed = (
        P("group", "blk", None),
        P(),
        P(),
        P("group", "blk", None),
        P("group", "blk", None),
        P("group", "blk"),
        P("group", "blk"),
        P(),
        P(),
        P(),
    )
    return jax.shard_map(
        functools.partial(on_device, mesh.shape["blk"], mesh.shape["group"]),
        mesh=mesh,
        in_specs=placed,
        out_specs=(P("group", "blk", None), P("group", "blk", None), P(), P(), P()),
        check_vma=False,
    )
```

```python
import functools

import jax
import jax.numpy as jnp
from jax import lax
from jax.experimental import pallas as pl
from jax.experimental.pallas import tpu as pltpu
from jax.sharding import PartitionSpec as P

EPSILON = 1e-06
GELU_SCALE = 0.7978845608028654
GELU_CUBE = 0.044715
LANES = 128
VMEM_LIMIT = 32 * 1024 * 1024
F32 = jnp.float32
BF16 = jnp.bfloat16

VMEM = pl.BlockSpec(memory_space=pltpu.VMEM)
SMEM = pl.BlockSpec(memory_space=pltpu.SMEM)
HBM = pl.BlockSpec(memory_space=pltpu.HBM)


def params():
    return pltpu.CompilerParams(vmem_limit_bytes=VMEM_LIMIT)


def three_parts(values):
    high = values.astype(BF16).astype(F32)
    rest = values - high
    middle = rest.astype(BF16).astype(F32)
    return high, middle, rest - middle


def rows_to_column(row, count):
    here = lax.broadcasted_iota(jnp.int32, (count, count), 0)
    there = lax.broadcasted_iota(jnp.int32, (count, count), 1)
    return jnp.sum(jnp.where(here == there, row, 0.0), axis=1, keepdims=True)


def forward_kernel(
    tokens_hbm,
    gain_hbm,
    weight_hbm,
    lengths_hbm,
    positives_hbm,
    sample_hbm,
    send_hbm,
    slope_ref,
    pooled_ref,
    tokens_ref,
    gain_ref,
    weight_ref,
    lengths_ref,
    positives_ref,
    sample_ref,
    normed_ref,
    own_ref,
    small_sems,
    token_sems,
    weight_sems,
    send_sems,
):
    sketches = lengths_ref.shape[-1]
    tok_count, depth = tokens_ref.shape
    features = weight_ref.shape[1]
    token_parts, weight_parts = token_sems.shape[0], weight_sems.shape[0]
    block, width = tok_count // token_parts, features // weight_parts

    small = [
        pltpu.make_async_copy(source, target, small_sems.at[i])
        for i, (source, target) in enumerate(
            (
                (gain_hbm, gain_ref),
                (lengths_hbm, lengths_ref),
                (positives_hbm, positives_ref),
                (sample_hbm, sample_ref),
            )
        )
    ]
    token_copies = [
        pltpu.make_async_copy(
            tokens_hbm.at[0, pl.ds(i * block, block)], tokens_ref.at[pl.ds(i * block, block)], token_sems.at[i]
        )
        for i in range(token_parts)
    ]
    weight_copies = [
        pltpu.make_async_copy(
            weight_hbm.at[:, pl.ds(i * width, width)], weight_ref.at[:, pl.ds(i * width, width)], weight_sems.at[i]
        )
        for i in range(weight_parts)
    ]
    small[0].start()
    for copy in token_copies:
        copy.start()
    for copy in small[1:]:
        copy.start()
    for copy in weight_copies:
        copy.start()

    small[0].wait()
    gain = gain_ref[...]
    for i, copy in enumerate(token_copies):
        copy.wait()
        rows = pl.ds(i * block, block)
        inputs = tokens_ref[rows].astype(F32)
        inv_rms = lax.rsqrt(jnp.mean(inputs * inputs, axis=-1, keepdims=True) + EPSILON)
        normed_ref[rows] = (inputs * inv_rms * gain).astype(BF16)

    for copy in small[1:]:
        copy.wait()
    lens_row = lengths_ref[0].astype(F32)
    lens_col = rows_to_column(lens_row, sketches)
    here = lax.broadcasted_iota(jnp.int32, (sketches, sketches), 0)
    there = lax.broadcasted_iota(jnp.int32, (sketches, sketches), 1)
    ends = jnp.sum(jnp.where(there <= here, lens_row, 0.0), axis=1, keepdims=True)
    place = lax.broadcasted_iota(jnp.int32, (sketches, tok_count), 1).astype(F32)
    membership = jnp.where((place < ends) & (place >= ends - lens_col), 1.0, 0.0).astype(BF16)

    for i, copy in enumerate(weight_copies):
        copy.wait()
        columns = pl.ds(i * width, width)
        values = jnp.dot(normed_ref[...], weight_ref[:, columns], preferred_element_type=F32)
        square = values * values
        tanh_part = jnp.tanh(values * (GELU_SCALE + (GELU_SCALE * GELU_CUBE) * square))
        half = 0.5 + 0.5 * tanh_part
        activated = (values * half).astype(BF16)
        slope = half + values * (1.0 - tanh_part * tanh_part) * (
            0.5 * GELU_SCALE + (1.5 * GELU_SCALE * GELU_CUBE) * square
        )
        slope_ref[:, columns] = slope.astype(BF16)
        pooled_ref[:, columns] = jnp.dot(membership, activated, preferred_element_type=F32) / lens_col

    pooled = pooled_ref[...]
    rnorm = lax.rsqrt(jnp.sum(pooled * pooled, axis=-1, keepdims=True) + EPSILON)
    embed = (pooled * rnorm).astype(BF16)
    paired = rows_to_column(positives_ref[...].astype(F32), sketches)
    paired_high = jnp.floor(paired * (1.0 / 16.0))
    weight = three_parts(rows_to_column(sample_ref[...], sketches))
    lane = lax.broadcasted_iota(jnp.int32, (sketches, LANES), 1)
    extra = jnp.zeros((sketches, LANES), F32)
    for i, column in enumerate((paired_high, paired - 16.0 * paired_high) + weight):
        extra = jnp.where(lane == i, column, extra)
    own_ref[:, :features] = embed
    own_ref[:, features:] = extra.astype(BF16)
    send_copies = [
        pltpu.make_async_copy(own_ref, send_hbm.at[i], send_sems.at[i]) for i in range(send_hbm.shape[0])
    ]
    for copy in send_copies:
        copy.start()
    for copy in send_copies:
        copy.wait()


def score_kernel(
    inv_count,
    scalars_ref,
    place_ref,
    sketch_hbm,
    near_ref,
    other_ref,
    back_hbm,
    near_out_ref,
    other_out_hbm,
    sketch_ref,
    back_ref,
    other_out_ref,
    in_sem,
    out_sems,
):
    members, sketches = sketch_ref.shape[:2]
    far, _, features = near_ref.shape
    halves = 2
    rows, half = members * sketches, far * sketches
    texts = halves * half
    sketch_copy = pltpu.make_async_copy(sketch_hbm, sketch_ref, in_sem)
    sketch_copy.start()
    temper = jnp.exp(jnp.full((1, 1), scalars_ref[0], F32))
    column = lax.broadcasted_iota(jnp.int32, (1, texts), 1)
    first = jnp.zeros((1, texts), jnp.int32)
    for i in range(halves * far):
        first = jnp.where(column >= i * sketches, (place_ref[i] - i) * sketches, first)
    column = (column + first).astype(F32)
    text_in = jnp.concatenate(
        [ref[...].reshape(half, features) for ref in (near_ref, other_ref)], axis=0
    ).astype(F32)
    text_rnorm = lax.rsqrt(jnp.sum(text_in * text_in, axis=-1, keepdims=True) + EPSILON)
    text = (text_in * text_rnorm).astype(BF16)
    sketch_copy.wait()
    sketch = sketch_ref[:, :, :features].reshape(rows, features)
    extra = sketch_ref[:, :, features:].reshape(rows, LANES).astype(F32)
    paired = extra[:, 0:1] * 16.0 + extra[:, 1:2]
    weight = ((extra[:, 2:3] + extra[:, 3:4]) + extra[:, 4:5]) * inv_count
    dots = lax.dot_general(sketch, text, (((1,), (1,)), ((), ())), preferred_element_type=F32)
    logits = temper * dots + scalars_ref[1]
    is_pair = paired == column
    signs = jnp.where(is_pair, 1.0, -1.0)
    against = jnp.where(is_pair, -logits, logits)
    decay = jnp.exp(-jnp.abs(against))
    chance = jnp.where(against >= 0.0, 1.0, decay) / (1.0 + decay)
    coeffs = -weight * signs * chance
    scaled = (coeffs * (temper * scalars_ref[2])).astype(BF16)
    sketch_part = jnp.dot(scaled, text, preferred_element_type=F32).astype(BF16)
    back_ref[:, :, :features] = sketch_part.reshape(members, sketches, features)
    pair_loss = jnp.maximum(against, 0.0) + jnp.log1p(decay)

    def total(values):
        return jnp.sum(jnp.sum(values, axis=1, keepdims=True), axis=0, keepdims=True)

    lane = lax.broadcasted_iota(jnp.int32, (sketches, LANES), 1)
    sums = jnp.zeros((sketches, LANES), F32)
    for i, value in enumerate((total(weight * pair_loss), total(coeffs * temper * dots), total(coeffs))):
        for j, piece in enumerate(three_parts(value)):
            sums = jnp.where(lane == 3 * j + i, piece, sums)
    sums = sums.astype(BF16)
    for member in range(members):
        back_ref[member, :, features:] = sums
    back_copy = pltpu.make_async_copy(back_ref, back_hbm, out_sems.at[0])
    back_copy.start()
    text_part = lax.dot_general(scaled, sketch, (((0,), (0,)), ((), ())), preferred_element_type=F32)
    other_out_ref[...] = text_part[half:].astype(BF16).reshape(far, sketches, features)
    other_out_copy = pltpu.make_async_copy(other_out_ref, other_out_hbm, out_sems.at[1])
    other_out_copy.start()
    near_out_ref[...] = text_part[:half].reshape(far, sketches, features)
    back_copy.wait()
    other_out_copy.wait()


def backward_kernel(
    parts_ref,
    pooled_ref,
    slope_ref,
    lengths_hbm,
    tokens_hbm,
    gain_hbm,
    weight_hbm,
    out_hbm,
    lengths_ref,
    tokens_ref,
    gain_ref,
    weight_ref,
    act_ref,
    back_ref,
    out_ref,
    small_sems,
    token_sems,
    weight_sems,
    out_sems,
):
    sketches = lengths_ref.shape[-1]
    tok_count, depth = tokens_ref.shape
    features = slope_ref.shape[1]
    token_parts, weight_parts = token_sems.shape[0], weight_sems.shape[0]
    block, width = tok_count // token_parts, depth // weight_parts

    def rows(i):
        return pl.ds(i * block, block)

    def columns(i):
        return pl.ds(i * width, width)

    small = [
        pltpu.make_async_copy(lengths_hbm, lengths_ref, small_sems.at[0]),
        pltpu.make_async_copy(gain_hbm, gain_ref, small_sems.at[1]),
    ]
    weight_copies = [
        pltpu.make_async_copy(weight_hbm.at[columns(i)], weight_ref.at[columns(i)], weight_sems.at[i])
        for i in range(weight_parts)
    ]
    token_copies = [
        pltpu.make_async_copy(tokens_hbm.at[0, rows(i)], tokens_ref.at[rows(i)], token_sems.at[i])
        for i in range(token_parts)
    ]
    for copy in small + weight_copies + token_copies:
        copy.start()

    sketch_grad = jnp.sum(parts_ref[:, :, :features].astype(F32), axis=0)
    pooled = pooled_ref[...]
    rnorm = lax.rsqrt(jnp.sum(pooled * pooled, axis=-1, keepdims=True) + EPSILON)
    unit = pooled * rnorm
    along = jnp.sum(unit * sketch_grad, axis=-1, keepdims=True)
    for copy in small:
        copy.wait()
    lens_row = lengths_ref[0].astype(F32)
    lens_col = rows_to_column(lens_row, sketches)
    pool_grad = rnorm * (sketch_grad - unit * along) / lens_col
    high = pool_grad.astype(BF16)
    both = jnp.concatenate([high, (pool_grad - high.astype(F32)).astype(BF16)], axis=0)

    here = lax.broadcasted_iota(jnp.int32, (sketches, sketches), 0)
    there = lax.broadcasted_iota(jnp.int32, (sketches, sketches), 1)
    ends = jnp.sum(jnp.where(here <= there, lens_col, 0.0), axis=0, keepdims=True)
    place = lax.broadcasted_iota(jnp.int32, (tok_count, sketches), 0).astype(F32)
    membership = jnp.where((place < ends) & (place >= ends - lens_row), 1.0, 0.0).astype(BF16)
    membership = jnp.concatenate([membership, membership], axis=1)
    for i in range(token_parts):
        per_token = jnp.dot(membership[i * block : (i + 1) * block], both, preferred_element_type=F32)
        act_ref[rows(i)] = (per_token * slope_ref[rows(i)].astype(F32)).astype(BF16)

    for copy in token_copies:
        copy.wait()
    along_x = jnp.zeros((tok_count, 1), F32)
    power = jnp.zeros((tok_count, 1), F32)
    for i, copy in enumerate(weight_copies):
        copy.wait()
        grad = lax.dot_general(
            act_ref[...], weight_ref[columns(i)], (((1,), (1,)), ((), ())), preferred_element_type=F32
        )
        gain_part = grad * gain_ref[:, columns(i)]
        inputs = tokens_ref[:, columns(i)].astype(F32)
        back_ref[:, columns(i)] = gain_part
        along_x += jnp.sum(gain_part * inputs, axis=-1, keepdims=True)
        power += jnp.sum(inputs * inputs, axis=-1, keepdims=True)
    inv_rms = lax.rsqrt(power * (1.0 / depth) + EPSILON)
    shrink = inv_rms * inv_rms * inv_rms * (along_x * (1.0 / depth))
    out_copies = []
    for i in range(token_parts):
        span = slice(i * block, (i + 1) * block)
        inputs = tokens_ref[rows(i)].astype(F32)
        out_ref[rows(i)] = (inv_rms[span] * back_ref[rows(i)] - shrink[span] * inputs).astype(BF16)
        copy = pltpu.make_async_copy(out_ref.at[rows(i)], out_hbm.at[0, rows(i)], out_sems.at[i])
        copy.start()
        out_copies.append(copy)
    for copy in out_copies:
        copy.wait()


def on_device(cycle_size, cycles, tokens, norm_gain, proj_weight, text_feats, lengths, positives, sample_weight, log_temp, logit_bias, loss_scale):
    tok_count, depth = tokens.shape[1:]
    features = proj_weight.shape[1]
    sketches = text_feats.shape[1]
    far, near, members = lax.axis_size("far"), lax.axis_size("near"), lax.axis_size("col")
    inv_count = 1.0 / (cycles * cycle_size * sketches)
    wide = features + LANES

    def in_hbm(*values):
        return [pltpu.with_memory_space_constraint(value, pltpu.HBM) for value in values]

    def in_vmem(*values):
        return [pltpu.with_memory_space_constraint(value, pltpu.VMEM) for value in values]

    def partner(block):
        return lax.ppermute(block, "near", [(i, (i + 1) % near) for i in range(near)])

    text_send = jnp.broadcast_to(text_feats, (far, sketches, features))
    near_texts = lax.all_to_all(text_send, "far", 0, 0, tiled=True)

    gain, weights = norm_gain.reshape(1, depth), proj_weight
    token_parts, weight_parts = 4, 4
    sketch_send, slope, pooled = pl.pallas_call(
        forward_kernel,
        out_shape=(
            pltpu.HBM((members, sketches, wide), BF16),
            pltpu.VMEM((tok_count, features), BF16),
            pltpu.VMEM((sketches, features), F32),
        ),
        in_specs=[HBM] * 6,
        out_specs=(HBM, VMEM, VMEM),
        scratch_shapes=[
            pltpu.VMEM((tok_count, depth), BF16),
            pltpu.VMEM((1, depth), F32),
            pltpu.VMEM((depth, features), BF16),
            pltpu.VMEM((1, 1, sketches), jnp.int32),
            pltpu.VMEM((1, sketches), jnp.int32),
            pltpu.VMEM((1, sketches), F32),
            pltpu.VMEM((tok_count, depth), BF16),
            pltpu.VMEM((sketches, wide), BF16),
            pltpu.SemaphoreType.DMA((4,)),
            pltpu.SemaphoreType.DMA((token_parts,)),
            pltpu.SemaphoreType.DMA((weight_parts,)),
            pltpu.SemaphoreType.DMA((members,)),
        ],
        compiler_params=params(),
        cost_estimate=pl.CostEstimate(flops=2 * tok_count * depth * features, bytes_accessed=5 << 20, transcendentals=tok_count * features),
        name="forward",
    )(*in_hbm(tokens, gain, weights, lengths, positives, sample_weight))
    sketch_all = lax.all_to_all(sketch_send, "col", 0, 0, tiled=True)
    other_texts = partner(near_texts)

    far_place, near_place, col = lax.axis_index("far"), lax.axis_index("near"), lax.axis_index("col")
    place = jnp.stack(
        [(f * near + (near_place + h) % near) * members + col for h in range(near) for f in range(far)]
    ).astype(jnp.int32)
    scalars = jnp.stack([log_temp, logit_bias, loss_scale])
    sketch_parts, near_part, other_part = pl.pallas_call(
        functools.partial(score_kernel, inv_count),
        out_shape=(
            pltpu.HBM((members, sketches, wide), BF16),
            pltpu.VMEM((far, sketches, features), F32),
            pltpu.HBM((far, sketches, features), BF16),
        ),
        in_specs=[SMEM, SMEM, HBM, VMEM, VMEM],
        out_specs=(HBM, VMEM, HBM),
        scratch_shapes=[
            pltpu.VMEM((members, sketches, wide), BF16),
            pltpu.VMEM((members, sketches, wide), BF16),
            pltpu.VMEM((far, sketches, features), BF16),
            pltpu.SemaphoreType.DMA,
            pltpu.SemaphoreType.DMA((2,)),
        ],
        compiler_params=params(),
        name="score",
    )(scalars, place, *in_hbm(sketch_all), *in_vmem(near_texts, other_texts))
    sketch_back = lax.all_to_all(sketch_parts, "col", 0, 0, tiled=True)
    text_sum = (near_part + partner(other_part).astype(F32)).astype(BF16)

    def lane_sums(parts):
        found = jnp.sum(parts[:, 0, features : features + 9].astype(F32), axis=0)
        return found[0:3] + (found[3:6] + found[6:9])

    def rounded(values):
        return lax.reduce_precision(values, 8, 7)

    row_sums = lane_sums(sketch_back)
    high = rounded(row_sums)
    middle = rounded(row_sums - high)
    row_lanes = jnp.pad(jnp.concatenate([high, middle, row_sums - high - middle]), (0, LANES - 9)).astype(BF16)
    text_parts = jnp.concatenate([text_sum, jnp.broadcast_to(row_lanes, (far, sketches, LANES))], axis=2)
    text_back = lax.all_to_all(text_parts, "far", 0, 0, tiled=True)

    grad_tokens = pl.pallas_call(
        backward_kernel,
        out_shape=pltpu.HBM(tokens.shape, BF16),
        in_specs=[VMEM] * 3 + [HBM] * 4,
        out_specs=HBM,
        scratch_shapes=[
            pltpu.VMEM((1, 1, sketches), jnp.int32),
            pltpu.VMEM((tok_count, depth), BF16),
            pltpu.VMEM((1, depth), F32),
            pltpu.VMEM((depth, features), BF16),
            pltpu.VMEM((tok_count, features), BF16),
            pltpu.VMEM((tok_count, depth), F32),
            pltpu.VMEM((tok_count, depth), BF16),
            pltpu.SemaphoreType.DMA((2,)),
            pltpu.SemaphoreType.DMA((token_parts,)),
            pltpu.SemaphoreType.DMA((weight_parts,)),
            pltpu.SemaphoreType.DMA((token_parts,)),
        ],
        compiler_params=params(),
        cost_estimate=pl.CostEstimate(flops=2 * tok_count * depth * features, bytes_accessed=5 << 20, transcendentals=0),
        name="backward",
    )(sketch_back, *in_vmem(pooled, slope), *in_hbm(lengths, tokens, gain, weights))

    sums_send = jnp.broadcast_to(jnp.pad(lane_sums(text_back), (0, LANES - 3)), (near * cycles, 8, LANES))
    sums_all = lax.all_to_all(sums_send, ("near", "group"), 0, 0, tiled=True)
    sums = jnp.sum(sums_all[:, 0, :3], axis=0)

    text_grad = jnp.sum(text_back[:, :, :features].astype(F32), axis=0, keepdims=True)
    text_in = text_feats.astype(F32)
    rnorm = lax.rsqrt(jnp.sum(text_in * text_in, axis=-1, keepdims=True) + EPSILON)
    unit = text_in * rnorm
    along = jnp.sum(unit * text_grad, axis=-1, keepdims=True)
    grad_texts = rnorm * (text_grad - unit * along)
    return (grad_tokens, grad_texts, sums[0], sums[1], sums[2])


def solution(mesh):
    cycle_size, cycles = mesh.shape["blk"], mesh.shape["group"]
    far, near = 4, 2
    tiles = jax.sharding.Mesh(
        mesh.devices.reshape(far, near, cycle_size // (far * near), cycles), ("far", "near", "col", "group")
    )
    blk = ("far", "near", "col")
    placed = (
        P("group", blk, None),
        P(),
        P(),
        P("group", blk, None),
        P("group", blk, None),
        P("group", blk),
        P("group", blk),
        P(),
        P(),
        P(),
    )
    return jax.shard_map(
        functools.partial(on_device, cycle_size, cycles),
        mesh=tiles,
        in_specs=placed,
        out_specs=(P("group", blk, None), P("group", blk, None), P(), P(), P()),
        check_vma=False,
    )
```

```python
import functools

import jax
import jax.numpy as jnp
from jax import lax
from jax.experimental import pallas as pl
from jax.experimental.pallas import tpu as pltpu
from jax.sharding import PartitionSpec as P

EPSILON = 1e-06
GELU_SCALE = 0.7978845608028654
GELU_CUBE = 0.044715
LANES = 128
VMEM_LIMIT = 32 * 1024 * 1024
F32 = jnp.float32
BF16 = jnp.bfloat16

VMEM = pl.BlockSpec(memory_space=pltpu.VMEM)
SMEM = pl.BlockSpec(memory_space=pltpu.SMEM)
HBM = pl.BlockSpec(memory_space=pltpu.HBM)


def params():
    return pltpu.CompilerParams(vmem_limit_bytes=VMEM_LIMIT)


def three_parts(values):
    high = values.astype(BF16).astype(F32)
    rest = values - high
    middle = rest.astype(BF16).astype(F32)
    return high, middle, rest - middle


def rows_to_column(row, count):
    here = lax.broadcasted_iota(jnp.int32, (count, count), 0)
    there = lax.broadcasted_iota(jnp.int32, (count, count), 1)
    return jnp.sum(jnp.where(here == there, row, 0.0), axis=1, keepdims=True)


def forward_kernel(
    tokens_hbm,
    gain_hbm,
    weight_hbm,
    lengths_hbm,
    positives_hbm,
    sample_hbm,
    send_hbm,
    slope_ref,
    pooled_ref,
    tokens_ref,
    gain_ref,
    weight_ref,
    lengths_ref,
    positives_ref,
    sample_ref,
    normed_ref,
    own_ref,
    small_sems,
    token_sems,
    weight_sems,
    send_sems,
):
    sketches = lengths_ref.shape[-1]
    tok_count, depth = tokens_ref.shape
    features = weight_ref.shape[1]
    token_parts, weight_parts = token_sems.shape[0], weight_sems.shape[0]
    block, width = tok_count // token_parts, features // weight_parts

    small = [
        pltpu.make_async_copy(source, target, small_sems.at[i])
        for i, (source, target) in enumerate(
            (
                (gain_hbm, gain_ref),
                (lengths_hbm, lengths_ref),
                (positives_hbm, positives_ref),
                (sample_hbm, sample_ref),
            )
        )
    ]
    token_copies = [
        pltpu.make_async_copy(
            tokens_hbm.at[0, pl.ds(i * block, block)], tokens_ref.at[pl.ds(i * block, block)], token_sems.at[i]
        )
        for i in range(token_parts)
    ]
    weight_copies = [
        pltpu.make_async_copy(
            weight_hbm.at[:, pl.ds(i * width, width)], weight_ref.at[:, pl.ds(i * width, width)], weight_sems.at[i]
        )
        for i in range(weight_parts)
    ]
    small[0].start()
    for copy in token_copies:
        copy.start()
    for copy in small[1:]:
        copy.start()
    for copy in weight_copies:
        copy.start()

    small[0].wait()
    gain = gain_ref[...]
    for i, copy in enumerate(token_copies):
        copy.wait()
        rows = pl.ds(i * block, block)
        inputs = tokens_ref[rows].astype(F32)
        inv_rms = lax.rsqrt(jnp.mean(inputs * inputs, axis=-1, keepdims=True) + EPSILON)
        normed_ref[rows] = (inputs * inv_rms * gain).astype(BF16)

    for copy in small[1:]:
        copy.wait()
    lens_row = lengths_ref[0].astype(F32)
    lens_col = rows_to_column(lens_row, sketches)
    here = lax.broadcasted_iota(jnp.int32, (sketches, sketches), 0)
    there = lax.broadcasted_iota(jnp.int32, (sketches, sketches), 1)
    ends = jnp.sum(jnp.where(there <= here, lens_row, 0.0), axis=1, keepdims=True)
    place = lax.broadcasted_iota(jnp.int32, (sketches, tok_count), 1).astype(F32)
    membership = jnp.where((place < ends) & (place >= ends - lens_col), 1.0, 0.0).astype(BF16)

    for i, copy in enumerate(weight_copies):
        copy.wait()
        columns = pl.ds(i * width, width)
        values = jnp.dot(normed_ref[...], weight_ref[:, columns], preferred_element_type=F32)
        square = values * values
        tanh_part = jnp.tanh(values * (GELU_SCALE + (GELU_SCALE * GELU_CUBE) * square))
        half = 0.5 + 0.5 * tanh_part
        activated = (values * half).astype(BF16)
        slope = half + values * (1.0 - tanh_part * tanh_part) * (
            0.5 * GELU_SCALE + (1.5 * GELU_SCALE * GELU_CUBE) * square
        )
        slope_ref[:, columns] = slope.astype(BF16)
        pooled_ref[:, columns] = jnp.dot(membership, activated, preferred_element_type=F32) / lens_col

    pooled = pooled_ref[...]
    rnorm = lax.rsqrt(jnp.sum(pooled * pooled, axis=-1, keepdims=True) + EPSILON)
    embed = (pooled * rnorm).astype(BF16)
    paired = rows_to_column(positives_ref[...].astype(F32), sketches)
    paired_high = jnp.floor(paired * (1.0 / 16.0))
    weight = three_parts(rows_to_column(sample_ref[...], sketches))
    lane = lax.broadcasted_iota(jnp.int32, (sketches, LANES), 1)
    extra = jnp.zeros((sketches, LANES), F32)
    for i, column in enumerate((paired_high, paired - 16.0 * paired_high) + weight):
        extra = jnp.where(lane == i, column, extra)
    own_ref[:, :features] = embed
    own_ref[:, features:] = extra.astype(BF16)
    send_copies = [
        pltpu.make_async_copy(own_ref, send_hbm.at[i], send_sems.at[i]) for i in range(send_hbm.shape[0])
    ]
    for copy in send_copies:
        copy.start()
    for copy in send_copies:
        copy.wait()


def score_kernel(
    inv_count,
    scalars_ref,
    place_ref,
    sketch_ref,
    near_ref,
    other_ref,
    back_hbm,
    near_out_ref,
    other_out_hbm,
    back_ref,
    other_out_ref,
    out_sems,
):
    members, sketches = sketch_ref.shape[:2]
    far, _, features = near_ref.shape
    halves = 2
    rows, half = members * sketches, far * sketches
    texts = halves * half
    temper = jnp.exp(jnp.full((1, 1), scalars_ref[0], F32))
    column = lax.broadcasted_iota(jnp.int32, (1, texts), 1)
    first = jnp.zeros((1, texts), jnp.int32)
    for i in range(halves * far):
        first = jnp.where(column >= i * sketches, (place_ref[i] - i) * sketches, first)
    column = (column + first).astype(F32)
    text_in = jnp.concatenate(
        [ref[...].reshape(half, features) for ref in (near_ref, other_ref)], axis=0
    ).astype(F32)
    text_rnorm = lax.rsqrt(jnp.sum(text_in * text_in, axis=-1, keepdims=True) + EPSILON)
    text = (text_in * text_rnorm).astype(BF16)
    sketch = sketch_ref[:, :, :features].reshape(rows, features)
    extra = sketch_ref[:, :, features:].reshape(rows, LANES).astype(F32)
    paired = extra[:, 0:1] * 16.0 + extra[:, 1:2]
    weight = ((extra[:, 2:3] + extra[:, 3:4]) + extra[:, 4:5]) * inv_count
    dots = lax.dot_general(sketch, text, (((1,), (1,)), ((), ())), preferred_element_type=F32)
    logits = temper * dots + scalars_ref[1]
    is_pair = paired == column
    signs = jnp.where(is_pair, 1.0, -1.0)
    against = jnp.where(is_pair, -logits, logits)
    decay = jnp.exp(-jnp.abs(against))
    chance = jnp.where(against >= 0.0, 1.0, decay) / (1.0 + decay)
    coeffs = -weight * signs * chance
    scaled = (coeffs * (temper * scalars_ref[2])).astype(BF16)
    sketch_part = jnp.dot(scaled, text, preferred_element_type=F32).astype(BF16)
    back_ref[:, :, :features] = sketch_part.reshape(members, sketches, features)
    pair_loss = jnp.maximum(against, 0.0) + jnp.log1p(decay)

    def total(values):
        return jnp.sum(jnp.sum(values, axis=1, keepdims=True), axis=0, keepdims=True)

    lane = lax.broadcasted_iota(jnp.int32, (sketches, LANES), 1)
    sums = jnp.zeros((sketches, LANES), F32)
    for i, value in enumerate((total(weight * pair_loss), total(coeffs * temper * dots), total(coeffs))):
        for j, piece in enumerate(three_parts(value)):
            sums = jnp.where(lane == 3 * j + i, piece, sums)
    sums = sums.astype(BF16)
    for member in range(members):
        back_ref[member, :, features:] = sums
    back_copy = pltpu.make_async_copy(back_ref, back_hbm, out_sems.at[0])
    back_copy.start()
    text_part = lax.dot_general(scaled, sketch, (((0,), (0,)), ((), ())), preferred_element_type=F32)
    other_out_ref[...] = text_part[half:].astype(BF16).reshape(far, sketches, features)
    other_out_copy = pltpu.make_async_copy(other_out_ref, other_out_hbm, out_sems.at[1])
    other_out_copy.start()
    near_out_ref[...] = text_part[:half].reshape(far, sketches, features)
    back_copy.wait()
    other_out_copy.wait()


def backward_kernel(
    pooled_ref,
    slope_ref,
    parts_ref,
    lengths_hbm,
    tokens_hbm,
    gain_hbm,
    weight_hbm,
    out_hbm,
    lengths_ref,
    tokens_ref,
    gain_ref,
    weight_ref,
    act_ref,
    back_ref,
    out_ref,
    small_sems,
    token_sems,
    weight_sems,
    out_sems,
):
    sketches = lengths_ref.shape[-1]
    tok_count, depth = tokens_ref.shape
    features = slope_ref.shape[1]
    token_parts, weight_parts = token_sems.shape[0], weight_sems.shape[0]
    block, width = tok_count // token_parts, depth // weight_parts

    def rows(i):
        return pl.ds(i * block, block)

    def columns(i):
        return pl.ds(i * width, width)

    small = [
        pltpu.make_async_copy(lengths_hbm, lengths_ref, small_sems.at[0]),
        pltpu.make_async_copy(gain_hbm, gain_ref, small_sems.at[1]),
    ]
    weight_copies = [
        pltpu.make_async_copy(weight_hbm.at[columns(i)], weight_ref.at[columns(i)], weight_sems.at[i])
        for i in range(weight_parts)
    ]
    token_copies = [
        pltpu.make_async_copy(tokens_hbm.at[0, rows(i)], tokens_ref.at[rows(i)], token_sems.at[i])
        for i in range(token_parts)
    ]
    for copy in small + weight_copies + token_copies:
        copy.start()

    sketch_grad = jnp.sum(parts_ref[:, :, :features].astype(F32), axis=0)
    pooled = pooled_ref[...]
    rnorm = lax.rsqrt(jnp.sum(pooled * pooled, axis=-1, keepdims=True) + EPSILON)
    unit = pooled * rnorm
    along = jnp.sum(unit * sketch_grad, axis=-1, keepdims=True)
    for copy in small:
        copy.wait()
    lens_row = lengths_ref[0].astype(F32)
    lens_col = rows_to_column(lens_row, sketches)
    pool_grad = rnorm * (sketch_grad - unit * along) / lens_col
    high = pool_grad.astype(BF16)
    both = jnp.concatenate([high, (pool_grad - high.astype(F32)).astype(BF16)], axis=0)

    here = lax.broadcasted_iota(jnp.int32, (sketches, sketches), 0)
    there = lax.broadcasted_iota(jnp.int32, (sketches, sketches), 1)
    ends = jnp.sum(jnp.where(here <= there, lens_col, 0.0), axis=0, keepdims=True)
    place = lax.broadcasted_iota(jnp.int32, (tok_count, sketches), 0).astype(F32)
    membership = jnp.where((place < ends) & (place >= ends - lens_row), 1.0, 0.0).astype(BF16)
    membership = jnp.concatenate([membership, membership], axis=1)
    for i in range(token_parts):
        per_token = jnp.dot(membership[i * block : (i + 1) * block], both, preferred_element_type=F32)
        act_ref[rows(i)] = (per_token * slope_ref[rows(i)].astype(F32)).astype(BF16)

    for copy in token_copies:
        copy.wait()
    along_x = jnp.zeros((tok_count, 1), F32)
    power = jnp.zeros((tok_count, 1), F32)
    for i, copy in enumerate(weight_copies):
        copy.wait()
        grad = lax.dot_general(
            act_ref[...], weight_ref[columns(i)], (((1,), (1,)), ((), ())), preferred_element_type=F32
        )
        gain_part = grad * gain_ref[:, columns(i)]
        inputs = tokens_ref[:, columns(i)].astype(F32)
        back_ref[:, columns(i)] = gain_part
        along_x += jnp.sum(gain_part * inputs, axis=-1, keepdims=True)
        power += jnp.sum(inputs * inputs, axis=-1, keepdims=True)
    inv_rms = lax.rsqrt(power * (1.0 / depth) + EPSILON)
    shrink = inv_rms * inv_rms * inv_rms * (along_x * (1.0 / depth))
    out_copies = []
    for i in range(token_parts):
        span = slice(i * block, (i + 1) * block)
        inputs = tokens_ref[rows(i)].astype(F32)
        out_ref[rows(i)] = (inv_rms[span] * back_ref[rows(i)] - shrink[span] * inputs).astype(BF16)
        copy = pltpu.make_async_copy(out_ref.at[rows(i)], out_hbm.at[0, rows(i)], out_sems.at[i])
        copy.start()
        out_copies.append(copy)
    for copy in out_copies:
        copy.wait()


def text_grad_kernel(parts_ref, text_hbm, out_ref, text_ref, text_sem):
    copy = pltpu.make_async_copy(text_hbm.at[0], text_ref, text_sem)
    copy.start()
    text_grad = jnp.sum(parts_ref[:, :, : text_ref.shape[1]].astype(F32), axis=0)
    copy.wait()
    text_in = text_ref[...].astype(F32)
    rnorm = lax.rsqrt(jnp.sum(text_in * text_in, axis=-1, keepdims=True) + EPSILON)
    unit = text_in * rnorm
    along = jnp.sum(unit * text_grad, axis=-1, keepdims=True)
    out_ref[0] = rnorm * (text_grad - unit * along)


def on_device(cycle_size, cycles, tokens, norm_gain, proj_weight, text_feats, lengths, positives, sample_weight, log_temp, logit_bias, loss_scale):
    tok_count, depth = tokens.shape[1:]
    features = proj_weight.shape[1]
    sketches = text_feats.shape[1]
    far, near, members = lax.axis_size("far"), lax.axis_size("near"), lax.axis_size("col")
    inv_count = 1.0 / (cycles * cycle_size * sketches)
    wide = features + LANES

    def in_hbm(*values):
        return [pltpu.with_memory_space_constraint(value, pltpu.HBM) for value in values]

    def in_vmem(*values):
        return [pltpu.with_memory_space_constraint(value, pltpu.VMEM) for value in values]

    def partner(block):
        return lax.ppermute(block, "near", [(i, (i + 1) % near) for i in range(near)])

    text_send = jnp.broadcast_to(text_feats, (far, sketches, features))
    near_texts = lax.all_to_all(text_send, "far", 0, 0, tiled=True)

    gain, weights = norm_gain.reshape(1, depth), proj_weight
    token_parts, weight_parts = 4, 1
    sketch_send, slope, pooled = pl.pallas_call(
        forward_kernel,
        out_shape=(
            pltpu.HBM((members, sketches, wide), BF16),
            pltpu.VMEM((tok_count, features), BF16),
            pltpu.VMEM((sketches, features), F32),
        ),
        in_specs=[HBM] * 6,
        out_specs=(HBM, VMEM, VMEM),
        scratch_shapes=[
            pltpu.VMEM((tok_count, depth), BF16),
            pltpu.VMEM((1, depth), F32),
            pltpu.VMEM((depth, features), BF16),
            pltpu.VMEM((1, 1, sketches), jnp.int32),
            pltpu.VMEM((1, sketches), jnp.int32),
            pltpu.VMEM((1, sketches), F32),
            pltpu.VMEM((tok_count, depth), BF16),
            pltpu.VMEM((sketches, wide), BF16),
            pltpu.SemaphoreType.DMA((4,)),
            pltpu.SemaphoreType.DMA((token_parts,)),
            pltpu.SemaphoreType.DMA((weight_parts,)),
            pltpu.SemaphoreType.DMA((members,)),
        ],
        compiler_params=params(),
        cost_estimate=pl.CostEstimate(flops=2 * tok_count * depth * features, bytes_accessed=5 << 20, transcendentals=tok_count * features),
        name="forward",
    )(*in_hbm(tokens, gain, weights, lengths, positives, sample_weight))
    sketch_all = lax.all_to_all(sketch_send, "col", 0, 0, tiled=True)
    other_texts = partner(near_texts)

    far_place, near_place, col = lax.axis_index("far"), lax.axis_index("near"), lax.axis_index("col")
    place = jnp.stack(
        [(f * near + (near_place + h) % near) * members + col for h in range(near) for f in range(far)]
    ).astype(jnp.int32)
    scalars = jnp.stack([log_temp, logit_bias, loss_scale])
    sketch_parts, near_part, other_part = pl.pallas_call(
        functools.partial(score_kernel, inv_count),
        out_shape=(
            pltpu.HBM((members, sketches, wide), BF16),
            pltpu.VMEM((far, sketches, features), F32),
            pltpu.HBM((far, sketches, features), BF16),
        ),
        in_specs=[SMEM, SMEM, VMEM, VMEM, VMEM],
        out_specs=(HBM, VMEM, HBM),
        scratch_shapes=[
            pltpu.VMEM((members, sketches, wide), BF16),
            pltpu.VMEM((far, sketches, features), BF16),
            pltpu.SemaphoreType.DMA((2,)),
        ],
        compiler_params=params(),
        name="score",
    )(scalars, place, *in_vmem(sketch_all, near_texts, other_texts))
    sketch_back = lax.all_to_all(sketch_parts, "col", 0, 0, tiled=True)
    text_sum = (near_part + partner(other_part).astype(F32)).astype(BF16)

    def lane_sums(parts):
        found = jnp.sum(parts[:, 0, features : features + 9].astype(F32), axis=0)
        return found[0:3] + (found[3:6] + found[6:9])

    def rounded(values):
        return lax.reduce_precision(values, 8, 7)

    row_sums = lane_sums(sketch_back)
    high = rounded(row_sums)
    middle = rounded(row_sums - high)
    row_lanes = jnp.pad(jnp.concatenate([high, middle, row_sums - high - middle]), (0, LANES - 9)).astype(BF16)
    text_parts = jnp.concatenate([text_sum, jnp.broadcast_to(row_lanes, (far, sketches, LANES))], axis=2)
    text_back = lax.all_to_all(text_parts, "far", 0, 0, tiled=True)

    grad_tokens = pl.pallas_call(
        backward_kernel,
        out_shape=pltpu.HBM(tokens.shape, BF16),
        in_specs=[VMEM] * 3 + [HBM] * 4,
        out_specs=HBM,
        scratch_shapes=[
            pltpu.VMEM((1, 1, sketches), jnp.int32),
            pltpu.VMEM((tok_count, depth), BF16),
            pltpu.VMEM((1, depth), F32),
            pltpu.VMEM((depth, features), BF16),
            pltpu.VMEM((tok_count, features), BF16),
            pltpu.VMEM((tok_count, depth), F32),
            pltpu.VMEM((tok_count, depth), BF16),
            pltpu.SemaphoreType.DMA((2,)),
            pltpu.SemaphoreType.DMA((token_parts,)),
            pltpu.SemaphoreType.DMA((weight_parts,)),
            pltpu.SemaphoreType.DMA((token_parts,)),
        ],
        compiler_params=params(),
        cost_estimate=pl.CostEstimate(flops=2 * tok_count * depth * features, bytes_accessed=5 << 20, transcendentals=0),
        name="backward",
    )(*in_vmem(pooled, slope, sketch_back), *in_hbm(lengths, tokens, gain, weights))
    sums_send = jnp.broadcast_to(jnp.pad(lane_sums(text_back), (0, LANES - 3)), (near * cycles, 8, LANES))
    sums_send, grad_tokens = lax.optimization_barrier((sums_send, grad_tokens))
    sums_all = lax.all_to_all(sums_send, ("near", "group"), 0, 0, tiled=True)
    sums = jnp.sum(sums_all[:, 0, :3], axis=0)

    grad_texts = pl.pallas_call(
        text_grad_kernel,
        out_shape=pltpu.HBM(text_feats.shape, F32),
        in_specs=[VMEM, HBM],
        out_specs=VMEM,
        scratch_shapes=[pltpu.VMEM((sketches, features), BF16), pltpu.SemaphoreType.DMA],
        name="text_grad",
    )(text_back, *in_hbm(text_feats))
    return (grad_tokens, grad_texts, sums[0], sums[1], sums[2])


def solution(mesh):
    cycle_size, cycles = mesh.shape["blk"], mesh.shape["group"]
    far, near = 4, 2
    tiles = jax.sharding.Mesh(
        mesh.devices.reshape(far, near, cycle_size // (far * near), cycles), ("far", "near", "col", "group")
    )
    blk = ("far", "near", "col")
    placed = (
        P("group", blk, None),
        P(),
        P(),
        P("group", blk, None),
        P("group", blk, None),
        P("group", blk),
        P("group", blk),
        P(),
        P(),
        P(),
    )
    return jax.shard_map(
        functools.partial(on_device, cycle_size, cycles),
        mesh=tiles,
        in_specs=placed,
        out_specs=(P("group", blk, None), P("group", blk, None), P(), P(), P()),
        check_vma=False,
    )
```

```python
import functools

import jax
import jax.numpy as jnp
from jax import lax
from jax.experimental import pallas as pl
from jax.experimental.pallas import tpu as pltpu
from jax.sharding import PartitionSpec as P

EPSILON = 1e-06
GELU_SCALE = 0.7978845608028654
GELU_CUBE = 0.044715
LANES = 128
VMEM_LIMIT = 32 * 1024 * 1024
F32 = jnp.float32
BF16 = jnp.bfloat16

VMEM = pl.BlockSpec(memory_space=pltpu.VMEM)
SMEM = pl.BlockSpec(memory_space=pltpu.SMEM)
HBM = pl.BlockSpec(memory_space=pltpu.HBM)


def params():
    return pltpu.CompilerParams(vmem_limit_bytes=VMEM_LIMIT)


def three_parts(values):
    high = values.astype(BF16).astype(F32)
    rest = values - high
    middle = rest.astype(BF16).astype(F32)
    return high, middle, rest - middle


def rows_to_column(row, count):
    here = lax.broadcasted_iota(jnp.int32, (count, count), 0)
    there = lax.broadcasted_iota(jnp.int32, (count, count), 1)
    return jnp.sum(jnp.where(here == there, row, 0.0), axis=1, keepdims=True)


def forward_kernel(
    tokens_hbm,
    gain_hbm,
    weight_hbm,
    lengths_hbm,
    positives_hbm,
    sample_hbm,
    send_hbm,
    preact_ref,
    pooled_ref,
    tokens_ref,
    gain_ref,
    weight_ref,
    lengths_ref,
    positives_ref,
    sample_ref,
    normed_ref,
    own_ref,
    small_sems,
    token_sems,
    weight_sems,
    send_sems,
):
    sketches = lengths_ref.shape[-1]
    tok_count, depth = tokens_ref.shape
    features = weight_ref.shape[1]
    token_parts, weight_parts = token_sems.shape[0], weight_sems.shape[0]
    block, width = tok_count // token_parts, features // weight_parts

    small = [
        pltpu.make_async_copy(source, target, small_sems.at[i])
        for i, (source, target) in enumerate(
            (
                (gain_hbm, gain_ref),
                (lengths_hbm, lengths_ref),
                (positives_hbm, positives_ref),
                (sample_hbm, sample_ref),
            )
        )
    ]
    token_copies = [
        pltpu.make_async_copy(
            tokens_hbm.at[0, pl.ds(i * block, block)], tokens_ref.at[pl.ds(i * block, block)], token_sems.at[i]
        )
        for i in range(token_parts)
    ]
    weight_copies = [
        pltpu.make_async_copy(
            weight_hbm.at[:, pl.ds(i * width, width)], weight_ref.at[:, pl.ds(i * width, width)], weight_sems.at[i]
        )
        for i in range(weight_parts)
    ]
    small[0].start()
    for copy in token_copies:
        copy.start()
    for copy in small[1:]:
        copy.start()
    for copy in weight_copies:
        copy.start()

    small[0].wait()
    gain = gain_ref[...]
    for i, copy in enumerate(token_copies):
        copy.wait()
        rows = pl.ds(i * block, block)
        inputs = tokens_ref[rows].astype(F32)
        inv_rms = lax.rsqrt(jnp.mean(inputs * inputs, axis=-1, keepdims=True) + EPSILON)
        normed_ref[rows] = (inputs * inv_rms * gain).astype(BF16)

    for copy in small[1:]:
        copy.wait()
    lens_row = lengths_ref[0].astype(F32)
    lens_col = rows_to_column(lens_row, sketches)
    here = lax.broadcasted_iota(jnp.int32, (sketches, sketches), 0)
    there = lax.broadcasted_iota(jnp.int32, (sketches, sketches), 1)
    ends = jnp.sum(jnp.where(there <= here, lens_row, 0.0), axis=1, keepdims=True)
    place = lax.broadcasted_iota(jnp.int32, (sketches, tok_count), 1).astype(F32)
    membership = jnp.where((place < ends) & (place >= ends - lens_col), 1.0, 0.0).astype(BF16)

    for i, copy in enumerate(weight_copies):
        copy.wait()
        columns = pl.ds(i * width, width)
        values = jnp.dot(normed_ref[...], weight_ref[:, columns], preferred_element_type=F32)
        square = values * values
        tanh_part = jnp.tanh(values * (GELU_SCALE + (GELU_SCALE * GELU_CUBE) * square))
        activated = (values * (0.5 + 0.5 * tanh_part)).astype(BF16)
        preact_ref[:, columns] = values.astype(BF16)
        pooled_ref[:, columns] = jnp.dot(membership, activated, preferred_element_type=F32) / lens_col

    pooled = pooled_ref[...]
    rnorm = lax.rsqrt(jnp.sum(pooled * pooled, axis=-1, keepdims=True) + EPSILON)
    embed = (pooled * rnorm).astype(BF16)
    paired = rows_to_column(positives_ref[...].astype(F32), sketches)
    paired_high = jnp.floor(paired * (1.0 / 16.0))
    weight = three_parts(rows_to_column(sample_ref[...], sketches))
    lane = lax.broadcasted_iota(jnp.int32, (sketches, LANES), 1)
    extra = jnp.zeros((sketches, LANES), F32)
    for i, column in enumerate((paired_high, paired - 16.0 * paired_high) + weight):
        extra = jnp.where(lane == i, column, extra)
    own_ref[:, :features] = embed
    own_ref[:, features:] = extra.astype(BF16)
    send_copies = [
        pltpu.make_async_copy(own_ref, send_hbm.at[i], send_sems.at[i]) for i in range(send_hbm.shape[0])
    ]
    for copy in send_copies:
        copy.start()
    for copy in send_copies:
        copy.wait()


def score_kernel(
    inv_count,
    scalars_ref,
    place_ref,
    sketch_ref,
    near_ref,
    other_ref,
    back_hbm,
    near_out_ref,
    other_out_hbm,
    back_ref,
    other_out_ref,
    out_sems,
):
    members, sketches = sketch_ref.shape[:2]
    far, _, features = near_ref.shape
    halves = 2
    rows, half = members * sketches, far * sketches
    texts = halves * half
    temper = jnp.exp(jnp.full((1, 1), scalars_ref[0], F32))
    column = lax.broadcasted_iota(jnp.int32, (1, texts), 1)
    first = jnp.zeros((1, texts), jnp.int32)
    for i in range(halves * far):
        first = jnp.where(column >= i * sketches, (place_ref[i] - i) * sketches, first)
    column = (column + first).astype(F32)
    text_in = jnp.concatenate(
        [ref[...].reshape(half, features) for ref in (near_ref, other_ref)], axis=0
    ).astype(F32)
    text_rnorm = lax.rsqrt(jnp.sum(text_in * text_in, axis=-1, keepdims=True) + EPSILON)
    text = (text_in * text_rnorm).astype(BF16)
    sketch = sketch_ref[:, :, :features].reshape(rows, features)
    extra = sketch_ref[:, :, features:].reshape(rows, LANES).astype(F32)
    paired = extra[:, 0:1] * 16.0 + extra[:, 1:2]
    weight = ((extra[:, 2:3] + extra[:, 3:4]) + extra[:, 4:5]) * inv_count
    dots = lax.dot_general(sketch, text, (((1,), (1,)), ((), ())), preferred_element_type=F32)
    logits = temper * dots + scalars_ref[1]
    is_pair = paired == column
    signs = jnp.where(is_pair, 1.0, -1.0)
    against = jnp.where(is_pair, -logits, logits)
    decay = jnp.exp(-jnp.abs(against))
    chance = jnp.where(against >= 0.0, 1.0, decay) / (1.0 + decay)
    coeffs = -weight * signs * chance
    scaled = (coeffs * (temper * scalars_ref[2])).astype(BF16)
    sketch_part = jnp.dot(scaled, text, preferred_element_type=F32).astype(BF16)
    back_ref[:, :, :features] = sketch_part.reshape(members, sketches, features)
    pair_loss = jnp.maximum(against, 0.0) + jnp.log1p(decay)

    def total(values):
        return jnp.sum(jnp.sum(values, axis=1, keepdims=True), axis=0, keepdims=True)

    lane = lax.broadcasted_iota(jnp.int32, (sketches, LANES), 1)
    sums = jnp.zeros((sketches, LANES), F32)
    for i, value in enumerate((total(weight * pair_loss), total(coeffs * temper * dots), total(coeffs))):
        for j, piece in enumerate(three_parts(value)):
            sums = jnp.where(lane == 3 * j + i, piece, sums)
    sums = sums.astype(BF16)
    for member in range(members):
        back_ref[member, :, features:] = sums
    back_copy = pltpu.make_async_copy(back_ref, back_hbm, out_sems.at[0])
    back_copy.start()
    text_part = lax.dot_general(scaled, sketch, (((0,), (0,)), ((), ())), preferred_element_type=F32)
    other_out_ref[...] = text_part[half:].astype(BF16).reshape(far, sketches, features)
    other_out_copy = pltpu.make_async_copy(other_out_ref, other_out_hbm, out_sems.at[1])
    other_out_copy.start()
    near_out_ref[...] = text_part[:half].reshape(far, sketches, features)
    back_copy.wait()
    other_out_copy.wait()


def backward_kernel(
    pooled_ref,
    preact_ref,
    parts_ref,
    lengths_hbm,
    tokens_hbm,
    gain_hbm,
    weight_hbm,
    out_hbm,
    lengths_ref,
    tokens_ref,
    gain_ref,
    weight_ref,
    act_ref,
    back_ref,
    out_ref,
    small_sems,
    token_sems,
    weight_sems,
    out_sems,
):
    sketches = lengths_ref.shape[-1]
    tok_count, depth = tokens_ref.shape
    features = preact_ref.shape[1]
    token_parts, weight_parts = token_sems.shape[0], weight_sems.shape[0]
    block, width = tok_count // token_parts, depth // weight_parts

    def rows(i):
        return pl.ds(i * block, block)

    def columns(i):
        return pl.ds(i * width, width)

    small = [
        pltpu.make_async_copy(lengths_hbm, lengths_ref, small_sems.at[0]),
        pltpu.make_async_copy(gain_hbm, gain_ref, small_sems.at[1]),
    ]
    weight_copies = [
        pltpu.make_async_copy(weight_hbm.at[columns(i)], weight_ref.at[columns(i)], weight_sems.at[i])
        for i in range(weight_parts)
    ]
    token_copies = [
        pltpu.make_async_copy(tokens_hbm.at[0, rows(i)], tokens_ref.at[rows(i)], token_sems.at[i])
        for i in range(token_parts)
    ]
    for copy in small + weight_copies + token_copies:
        copy.start()

    sketch_grad = jnp.sum(parts_ref[:, :, :features].astype(F32), axis=0)
    pooled = pooled_ref[...]
    rnorm = lax.rsqrt(jnp.sum(pooled * pooled, axis=-1, keepdims=True) + EPSILON)
    unit = pooled * rnorm
    along = jnp.sum(unit * sketch_grad, axis=-1, keepdims=True)
    for copy in small:
        copy.wait()
    lens_row = lengths_ref[0].astype(F32)
    lens_col = rows_to_column(lens_row, sketches)
    pool_grad = rnorm * (sketch_grad - unit * along) / lens_col
    high = pool_grad.astype(BF16)
    both = jnp.concatenate([high, (pool_grad - high.astype(F32)).astype(BF16)], axis=0)

    here = lax.broadcasted_iota(jnp.int32, (sketches, sketches), 0)
    there = lax.broadcasted_iota(jnp.int32, (sketches, sketches), 1)
    ends = jnp.sum(jnp.where(here <= there, lens_col, 0.0), axis=0, keepdims=True)
    place = lax.broadcasted_iota(jnp.int32, (tok_count, sketches), 0).astype(F32)
    membership = jnp.where((place < ends) & (place >= ends - lens_row), 1.0, 0.0).astype(BF16)
    membership = jnp.concatenate([membership, membership], axis=1)
    for i in range(token_parts):
        per_token = jnp.dot(membership[i * block : (i + 1) * block], both, preferred_element_type=F32)
        values = preact_ref[rows(i)].astype(F32)
        square = values * values
        tanh_part = jnp.tanh(values * (GELU_SCALE + (GELU_SCALE * GELU_CUBE) * square))
        slope = (0.5 + 0.5 * tanh_part) + values * (1.0 - tanh_part * tanh_part) * (
            0.5 * GELU_SCALE + (1.5 * GELU_SCALE * GELU_CUBE) * square
        )
        act_ref[rows(i)] = (per_token * slope).astype(BF16)

    for copy in token_copies:
        copy.wait()
    along_x = jnp.zeros((tok_count, 1), F32)
    power = jnp.zeros((tok_count, 1), F32)
    for i, copy in enumerate(weight_copies):
        copy.wait()
        grad = lax.dot_general(
            act_ref[...], weight_ref[columns(i)], (((1,), (1,)), ((), ())), preferred_element_type=F32
        )
        gain_part = grad * gain_ref[:, columns(i)]
        inputs = tokens_ref[:, columns(i)].astype(F32)
        back_ref[:, columns(i)] = gain_part
        along_x += jnp.sum(gain_part * inputs, axis=-1, keepdims=True)
        power += jnp.sum(inputs * inputs, axis=-1, keepdims=True)
    inv_rms = lax.rsqrt(power * (1.0 / depth) + EPSILON)
    shrink = inv_rms * inv_rms * inv_rms * (along_x * (1.0 / depth))
    out_copies = []
    for i in range(token_parts):
        span = slice(i * block, (i + 1) * block)
        inputs = tokens_ref[rows(i)].astype(F32)
        out_ref[rows(i)] = (inv_rms[span] * back_ref[rows(i)] - shrink[span] * inputs).astype(BF16)
        copy = pltpu.make_async_copy(out_ref.at[rows(i)], out_hbm.at[0, rows(i)], out_sems.at[i])
        copy.start()
        out_copies.append(copy)
    for copy in out_copies:
        copy.wait()


def text_grad_kernel(parts_ref, text_hbm, out_ref, text_ref, text_sem):
    copy = pltpu.make_async_copy(text_hbm.at[0], text_ref, text_sem)
    copy.start()
    text_grad = jnp.sum(parts_ref[:, :, : text_ref.shape[1]].astype(F32), axis=0)
    copy.wait()
    text_in = text_ref[...].astype(F32)
    rnorm = lax.rsqrt(jnp.sum(text_in * text_in, axis=-1, keepdims=True) + EPSILON)
    unit = text_in * rnorm
    along = jnp.sum(unit * text_grad, axis=-1, keepdims=True)
    out_ref[0] = rnorm * (text_grad - unit * along)


def on_device(cycle_size, cycles, tokens, norm_gain, proj_weight, text_feats, lengths, positives, sample_weight, log_temp, logit_bias, loss_scale):
    tok_count, depth = tokens.shape[1:]
    features = proj_weight.shape[1]
    sketches = text_feats.shape[1]
    far, near, members = lax.axis_size("far"), lax.axis_size("near"), lax.axis_size("col")
    inv_count = 1.0 / (cycles * cycle_size * sketches)
    wide = features + LANES

    def in_hbm(*values):
        return [pltpu.with_memory_space_constraint(value, pltpu.HBM) for value in values]

    def in_vmem(*values):
        return [pltpu.with_memory_space_constraint(value, pltpu.VMEM) for value in values]

    def partner(block):
        return lax.ppermute(block, "near", [(i, (i + 1) % near) for i in range(near)])

    text_send = jnp.broadcast_to(text_feats, (far, sketches, features))
    near_texts = lax.all_to_all(text_send, "far", 0, 0, tiled=True)

    gain, weights = norm_gain.reshape(1, depth), proj_weight
    token_parts, weight_parts = 4, 1
    sketch_send, preact, pooled = pl.pallas_call(
        forward_kernel,
        out_shape=(
            pltpu.HBM((members, sketches, wide), BF16),
            pltpu.VMEM((tok_count, features), BF16),
            pltpu.VMEM((sketches, features), F32),
        ),
        in_specs=[HBM] * 6,
        out_specs=(HBM, VMEM, VMEM),
        scratch_shapes=[
            pltpu.VMEM((tok_count, depth), BF16),
            pltpu.VMEM((1, depth), F32),
            pltpu.VMEM((depth, features), BF16),
            pltpu.VMEM((1, 1, sketches), jnp.int32),
            pltpu.VMEM((1, sketches), jnp.int32),
            pltpu.VMEM((1, sketches), F32),
            pltpu.VMEM((tok_count, depth), BF16),
            pltpu.VMEM((sketches, wide), BF16),
            pltpu.SemaphoreType.DMA((4,)),
            pltpu.SemaphoreType.DMA((token_parts,)),
            pltpu.SemaphoreType.DMA((weight_parts,)),
            pltpu.SemaphoreType.DMA((members,)),
        ],
        compiler_params=params(),
        cost_estimate=pl.CostEstimate(flops=2 * tok_count * depth * features, bytes_accessed=5 << 20, transcendentals=tok_count * features),
        name="forward",
    )(*in_hbm(tokens, gain, weights, lengths, positives, sample_weight))
    sketch_all = lax.all_to_all(sketch_send, "col", 0, 0, tiled=True)
    other_texts = partner(near_texts)

    far_place, near_place, col = lax.axis_index("far"), lax.axis_index("near"), lax.axis_index("col")
    place = jnp.stack(
        [(f * members + col) * near + (near_place + h) % near for h in range(near) for f in range(far)]
    ).astype(jnp.int32)
    scalars = jnp.stack([log_temp, logit_bias, loss_scale])
    sketch_parts, near_part, other_part = pl.pallas_call(
        functools.partial(score_kernel, inv_count),
        out_shape=(
            pltpu.HBM((members, sketches, wide), BF16),
            pltpu.VMEM((far, sketches, features), F32),
            pltpu.HBM((far, sketches, features), BF16),
        ),
        in_specs=[SMEM, SMEM, VMEM, VMEM, VMEM],
        out_specs=(HBM, VMEM, HBM),
        scratch_shapes=[
            pltpu.VMEM((members, sketches, wide), BF16),
            pltpu.VMEM((far, sketches, features), BF16),
            pltpu.SemaphoreType.DMA((2,)),
        ],
        compiler_params=params(),
        name="score",
    )(scalars, place, *in_vmem(sketch_all, near_texts, other_texts))
    sketch_back = lax.all_to_all(sketch_parts, "col", 0, 0, tiled=True)
    text_sum = (near_part + partner(other_part).astype(F32)).astype(BF16)

    def lane_sums(parts):
        found = jnp.sum(parts[:, 0, features : features + 9].astype(F32), axis=0)
        return found[0:3] + (found[3:6] + found[6:9])

    def rounded(values):
        return lax.reduce_precision(values, 8, 7)

    row_sums = lane_sums(sketch_back)
    high = rounded(row_sums)
    middle = rounded(row_sums - high)
    row_lanes = jnp.pad(jnp.concatenate([high, middle, row_sums - high - middle]), (0, LANES - 9)).astype(BF16)
    text_parts = jnp.concatenate([text_sum, jnp.broadcast_to(row_lanes, (far, sketches, LANES))], axis=2)
    text_back = lax.all_to_all(text_parts, "far", 0, 0, tiled=True)

    grad_tokens = pl.pallas_call(
        backward_kernel,
        out_shape=pltpu.HBM(tokens.shape, BF16),
        in_specs=[VMEM] * 3 + [HBM] * 4,
        out_specs=HBM,
        scratch_shapes=[
            pltpu.VMEM((1, 1, sketches), jnp.int32),
            pltpu.VMEM((tok_count, depth), BF16),
            pltpu.VMEM((1, depth), F32),
            pltpu.VMEM((depth, features), BF16),
            pltpu.VMEM((tok_count, features), BF16),
            pltpu.VMEM((tok_count, depth), F32),
            pltpu.VMEM((tok_count, depth), BF16),
            pltpu.SemaphoreType.DMA((2,)),
            pltpu.SemaphoreType.DMA((token_parts,)),
            pltpu.SemaphoreType.DMA((weight_parts,)),
            pltpu.SemaphoreType.DMA((token_parts,)),
        ],
        compiler_params=params(),
        cost_estimate=pl.CostEstimate(flops=2 * tok_count * depth * features, bytes_accessed=5 << 20, transcendentals=0),
        name="backward",
    )(*in_vmem(pooled, preact, sketch_back), *in_hbm(lengths, tokens, gain, weights))
    sums_send = jnp.broadcast_to(jnp.pad(lane_sums(text_back), (0, LANES - 3)), (near * cycles, 8, LANES))
    sums_send, grad_tokens = lax.optimization_barrier((sums_send, grad_tokens))
    sums_all = lax.all_to_all(sums_send, ("near", "group"), 0, 0, tiled=True)
    sums = jnp.sum(sums_all[:, 0, :3], axis=0)

    grad_texts = pl.pallas_call(
        text_grad_kernel,
        out_shape=pltpu.HBM(text_feats.shape, F32),
        in_specs=[VMEM, HBM],
        out_specs=VMEM,
        scratch_shapes=[pltpu.VMEM((sketches, features), BF16), pltpu.SemaphoreType.DMA],
        name="text_grad",
    )(text_back, *in_hbm(text_feats))
    return (grad_tokens, grad_texts, sums[0], sums[1], sums[2])


def solution(mesh):
    cycle_size, cycles = mesh.shape["blk"], mesh.shape["group"]
    far, near = 4, 2
    tiles = jax.sharding.Mesh(
        mesh.devices.reshape(far, cycle_size // (far * near), near, cycles), ("far", "col", "near", "group")
    )
    blk = ("far", "col", "near")
    placed = (
        P("group", blk, None),
        P(),
        P(),
        P("group", blk, None),
        P("group", blk, None),
        P("group", blk),
        P("group", blk),
        P(),
        P(),
        P(),
    )
    return jax.shard_map(
        functools.partial(on_device, cycle_size, cycles),
        mesh=tiles,
        in_specs=placed,
        out_specs=(P("group", blk, None), P("group", blk, None), P(), P(), P()),
        check_vma=False,
    )
```

```python
import functools

import jax
import jax.numpy as jnp
from jax import lax
from jax.experimental import pallas as pl
from jax.experimental.pallas import tpu as pltpu
from jax.sharding import PartitionSpec as P

EPSILON = 1e-06
GELU_SCALE = 0.7978845608028654
GELU_CUBE = 0.044715
LANES = 128
VMEM_LIMIT = 32 * 1024 * 1024
F32 = jnp.float32
BF16 = jnp.bfloat16

VMEM = pl.BlockSpec(memory_space=pltpu.VMEM)
SMEM = pl.BlockSpec(memory_space=pltpu.SMEM)
HBM = pl.BlockSpec(memory_space=pltpu.HBM)


def params():
    return pltpu.CompilerParams(vmem_limit_bytes=VMEM_LIMIT)


def three_parts(values):
    high = values.astype(BF16).astype(F32)
    rest = values - high
    middle = rest.astype(BF16).astype(F32)
    return high, middle, rest - middle


def rows_to_column(row, count):
    here = lax.broadcasted_iota(jnp.int32, (count, count), 0)
    there = lax.broadcasted_iota(jnp.int32, (count, count), 1)
    return jnp.sum(jnp.where(here == there, row, 0.0), axis=1, keepdims=True)


def forward_kernel(
    tokens_hbm,
    gain_hbm,
    weight_hbm,
    lengths_hbm,
    positives_hbm,
    sample_hbm,
    send_hbm,
    preact_ref,
    pooled_ref,
    tokens_ref,
    gain_ref,
    weight_ref,
    lengths_ref,
    positives_ref,
    sample_ref,
    normed_ref,
    own_ref,
    small_sems,
    token_sems,
    weight_sems,
    send_sems,
):
    sketches = lengths_ref.shape[-1]
    tok_count, depth = tokens_ref.shape
    features = weight_ref.shape[1]
    token_parts, weight_parts = token_sems.shape[0], weight_sems.shape[0]
    block, width = tok_count // token_parts, features // weight_parts

    small = [
        pltpu.make_async_copy(source, target, small_sems.at[i])
        for i, (source, target) in enumerate(
            (
                (gain_hbm, gain_ref),
                (lengths_hbm, lengths_ref),
                (positives_hbm, positives_ref),
                (sample_hbm, sample_ref),
            )
        )
    ]
    token_copies = [
        pltpu.make_async_copy(
            tokens_hbm.at[0, pl.ds(i * block, block)], tokens_ref.at[pl.ds(i * block, block)], token_sems.at[i]
        )
        for i in range(token_parts)
    ]
    weight_copies = [
        pltpu.make_async_copy(
            weight_hbm.at[:, pl.ds(i * width, width)], weight_ref.at[:, pl.ds(i * width, width)], weight_sems.at[i]
        )
        for i in range(weight_parts)
    ]
    small[0].start()
    for copy in token_copies:
        copy.start()
    for copy in small[1:]:
        copy.start()
    for copy in weight_copies:
        copy.start()

    small[0].wait()
    gain = gain_ref[...]
    for i, copy in enumerate(token_copies):
        copy.wait()
        rows = pl.ds(i * block, block)
        inputs = tokens_ref[rows].astype(F32)
        inv_rms = lax.rsqrt(jnp.mean(inputs * inputs, axis=-1, keepdims=True) + EPSILON)
        normed_ref[rows] = (inputs * inv_rms * gain).astype(BF16)

    for copy in small[1:]:
        copy.wait()
    lens_row = lengths_ref[0].astype(F32)
    lens_col = rows_to_column(lens_row, sketches)
    here = lax.broadcasted_iota(jnp.int32, (sketches, sketches), 0)
    there = lax.broadcasted_iota(jnp.int32, (sketches, sketches), 1)
    ends = jnp.sum(jnp.where(there <= here, lens_row, 0.0), axis=1, keepdims=True)
    place = lax.broadcasted_iota(jnp.int32, (sketches, tok_count), 1).astype(F32)
    membership = jnp.where((place < ends) & (place >= ends - lens_col), 1.0, 0.0).astype(BF16)

    for i, copy in enumerate(weight_copies):
        copy.wait()
        columns = pl.ds(i * width, width)
        values = jnp.dot(normed_ref[...], weight_ref[:, columns], preferred_element_type=F32)
        square = values * values
        tanh_part = jnp.tanh(values * (GELU_SCALE + (GELU_SCALE * GELU_CUBE) * square))
        activated = (values * (0.5 + 0.5 * tanh_part)).astype(BF16)
        preact_ref[:, columns] = values.astype(BF16)
        pooled_ref[:, columns] = jnp.dot(membership, activated, preferred_element_type=F32) / lens_col

    pooled = pooled_ref[...]
    rnorm = lax.rsqrt(jnp.sum(pooled * pooled, axis=-1, keepdims=True) + EPSILON)
    embed = (pooled * rnorm).astype(BF16)
    paired = rows_to_column(positives_ref[...].astype(F32), sketches)
    paired_high = jnp.floor(paired * (1.0 / 16.0))
    weight = three_parts(rows_to_column(sample_ref[...], sketches))
    lane = lax.broadcasted_iota(jnp.int32, (sketches, LANES), 1)
    extra = jnp.zeros((sketches, LANES), F32)
    for i, column in enumerate((paired_high, paired - 16.0 * paired_high) + weight):
        extra = jnp.where(lane == i, column, extra)
    own_ref[:, :features] = embed
    own_ref[:, features:] = extra.astype(BF16)
    send_copies = [
        pltpu.make_async_copy(own_ref, send_hbm.at[i], send_sems.at[i]) for i in range(send_hbm.shape[0])
    ]
    for copy in send_copies:
        copy.start()
    for copy in send_copies:
        copy.wait()


def score_kernel(
    inv_count,
    scalars_ref,
    place_ref,
    sketch_ref,
    near_ref,
    other_ref,
    back_hbm,
    near_out_ref,
    other_out_ref,
    back_ref,
    out_sems,
):
    members, sketches = sketch_ref.shape[:2]
    far, _, features = near_ref.shape
    halves = 2
    rows, half = members * sketches, far * sketches
    texts = halves * half
    temper = jnp.exp(jnp.full((1, 1), scalars_ref[0], F32))
    column = lax.broadcasted_iota(jnp.int32, (1, texts), 1)
    first = jnp.zeros((1, texts), jnp.int32)
    for i in range(halves * far):
        first = jnp.where(column >= i * sketches, (place_ref[i] - i) * sketches, first)
    column = (column + first).astype(F32)
    text_in = jnp.concatenate(
        [ref[...].reshape(half, features) for ref in (near_ref, other_ref)], axis=0
    ).astype(F32)
    text_rnorm = lax.rsqrt(jnp.sum(text_in * text_in, axis=-1, keepdims=True) + EPSILON)
    text = (text_in * text_rnorm).astype(BF16)
    sketch = sketch_ref[:, :, :features].reshape(rows, features)
    extra = sketch_ref[:, :, features:].reshape(rows, LANES).astype(F32)
    paired = extra[:, 0:1] * 16.0 + extra[:, 1:2]
    weight = ((extra[:, 2:3] + extra[:, 3:4]) + extra[:, 4:5]) * inv_count
    dots = lax.dot_general(sketch, text, (((1,), (1,)), ((), ())), preferred_element_type=F32)
    logits = temper * dots + scalars_ref[1]
    is_pair = paired == column
    signs = jnp.where(is_pair, 1.0, -1.0)
    against = jnp.where(is_pair, -logits, logits)
    decay = jnp.exp(-jnp.abs(against))
    chance = jnp.where(against >= 0.0, 1.0, decay) / (1.0 + decay)
    coeffs = -weight * signs * chance
    scaled = (coeffs * (temper * scalars_ref[2])).astype(BF16)
    sketch_part = jnp.dot(scaled, text, preferred_element_type=F32).astype(BF16)
    back_ref[:, :, :features] = sketch_part.reshape(members, sketches, features)
    main = (slice(None), slice(None), pl.ds(0, features))
    lanes = (slice(None), slice(None), pl.ds(features, LANES))
    main_copy = pltpu.make_async_copy(back_ref.at[main], back_hbm.at[main], out_sems.at[0])
    main_copy.start()
    pair_loss = jnp.maximum(against, 0.0) + jnp.log1p(decay)

    def total(values):
        return jnp.sum(jnp.sum(values, axis=1, keepdims=True), axis=0, keepdims=True)

    lane = lax.broadcasted_iota(jnp.int32, (sketches, LANES), 1)
    sums = jnp.zeros((sketches, LANES), F32)
    for i, value in enumerate((total(weight * pair_loss), total(coeffs * temper * dots), total(coeffs))):
        for j, piece in enumerate(three_parts(value)):
            sums = jnp.where(lane == 3 * j + i, piece, sums)
    sums = sums.astype(BF16)
    for member in range(members):
        back_ref[member, :, features:] = sums
    lanes_copy = pltpu.make_async_copy(back_ref.at[lanes], back_hbm.at[lanes], out_sems.at[1])
    lanes_copy.start()
    text_part = lax.dot_general(scaled, sketch, (((0,), (0,)), ((), ())), preferred_element_type=F32)
    near_out_ref[...] = text_part[:half].reshape(far, sketches, features)
    other_out_ref[...] = text_part[half:].astype(BF16).reshape(far, sketches, features)
    main_copy.wait()
    lanes_copy.wait()


def backward_kernel(
    pooled_ref,
    preact_ref,
    parts_ref,
    lengths_hbm,
    tokens_hbm,
    gain_hbm,
    weight_hbm,
    out_hbm,
    lengths_ref,
    tokens_ref,
    gain_ref,
    weight_ref,
    act_ref,
    back_ref,
    out_ref,
    small_sems,
    token_sems,
    weight_sems,
    out_sems,
):
    sketches = lengths_ref.shape[-1]
    tok_count, depth = tokens_ref.shape
    features = preact_ref.shape[1]
    token_parts, weight_parts = token_sems.shape[0], weight_sems.shape[0]
    block, width = tok_count // token_parts, depth // weight_parts

    def rows(i):
        return pl.ds(i * block, block)

    def columns(i):
        return pl.ds(i * width, width)

    small = [
        pltpu.make_async_copy(lengths_hbm, lengths_ref, small_sems.at[0]),
        pltpu.make_async_copy(gain_hbm, gain_ref, small_sems.at[1]),
    ]
    weight_copies = [
        pltpu.make_async_copy(weight_hbm.at[columns(i)], weight_ref.at[columns(i)], weight_sems.at[i])
        for i in range(weight_parts)
    ]
    token_copies = [
        pltpu.make_async_copy(tokens_hbm.at[0, rows(i)], tokens_ref.at[rows(i)], token_sems.at[i])
        for i in range(token_parts)
    ]
    for copy in small + weight_copies + token_copies:
        copy.start()

    sketch_grad = jnp.sum(parts_ref[:, :, :features].astype(F32), axis=0)
    pooled = pooled_ref[...]
    rnorm = lax.rsqrt(jnp.sum(pooled * pooled, axis=-1, keepdims=True) + EPSILON)
    unit = pooled * rnorm
    along = jnp.sum(unit * sketch_grad, axis=-1, keepdims=True)
    for copy in small:
        copy.wait()
    lens_row = lengths_ref[0].astype(F32)
    lens_col = rows_to_column(lens_row, sketches)
    pool_grad = rnorm * (sketch_grad - unit * along) / lens_col
    high = pool_grad.astype(BF16)
    both = jnp.concatenate([high, (pool_grad - high.astype(F32)).astype(BF16)], axis=0)

    here = lax.broadcasted_iota(jnp.int32, (sketches, sketches), 0)
    there = lax.broadcasted_iota(jnp.int32, (sketches, sketches), 1)
    ends = jnp.sum(jnp.where(here <= there, lens_col, 0.0), axis=0, keepdims=True)
    place = lax.broadcasted_iota(jnp.int32, (tok_count, sketches), 0).astype(F32)
    membership = jnp.where((place < ends) & (place >= ends - lens_row), 1.0, 0.0).astype(BF16)
    membership = jnp.concatenate([membership, membership], axis=1)
    for i in range(token_parts):
        per_token = jnp.dot(membership[i * block : (i + 1) * block], both, preferred_element_type=F32)
        values = preact_ref[rows(i)].astype(F32)
        square = values * values
        tanh_part = jnp.tanh(values * (GELU_SCALE + (GELU_SCALE * GELU_CUBE) * square))
        slope = (0.5 + 0.5 * tanh_part) + values * (1.0 - tanh_part * tanh_part) * (
            0.5 * GELU_SCALE + (1.5 * GELU_SCALE * GELU_CUBE) * square
        )
        act_ref[rows(i)] = (per_token * slope).astype(BF16)

    for copy in token_copies:
        copy.wait()
    along_x = jnp.zeros((tok_count, 1), F32)
    power = jnp.zeros((tok_count, 1), F32)
    for i, copy in enumerate(weight_copies):
        copy.wait()
        grad = lax.dot_general(
            act_ref[...], weight_ref[columns(i)], (((1,), (1,)), ((), ())), preferred_element_type=F32
        )
        gain_part = grad * gain_ref[:, columns(i)]
        inputs = tokens_ref[:, columns(i)].astype(F32)
        back_ref[:, columns(i)] = gain_part
        along_x += jnp.sum(gain_part * inputs, axis=-1, keepdims=True)
        power += jnp.sum(inputs * inputs, axis=-1, keepdims=True)
    inv_rms = lax.rsqrt(power * (1.0 / depth) + EPSILON)
    shrink = inv_rms * inv_rms * inv_rms * (along_x * (1.0 / depth))
    out_copies = []
    for i in range(token_parts):
        span = slice(i * block, (i + 1) * block)
        inputs = tokens_ref[rows(i)].astype(F32)
        out_ref[rows(i)] = (inv_rms[span] * back_ref[rows(i)] - shrink[span] * inputs).astype(BF16)
        copy = pltpu.make_async_copy(out_ref.at[rows(i)], out_hbm.at[0, rows(i)], out_sems.at[i])
        copy.start()
        out_copies.append(copy)
    for copy in out_copies:
        copy.wait()


def text_grad_kernel(parts_ref, text_hbm, out_ref, text_ref, text_sem):
    copy = pltpu.make_async_copy(text_hbm.at[0], text_ref, text_sem)
    copy.start()
    text_grad = jnp.sum(parts_ref[:, :, : text_ref.shape[1]].astype(F32), axis=0)
    copy.wait()
    text_in = text_ref[...].astype(F32)
    rnorm = lax.rsqrt(jnp.sum(text_in * text_in, axis=-1, keepdims=True) + EPSILON)
    unit = text_in * rnorm
    along = jnp.sum(unit * text_grad, axis=-1, keepdims=True)
    out_ref[0] = rnorm * (text_grad - unit * along)


def on_device(cycle_size, cycles, tokens, norm_gain, proj_weight, text_feats, lengths, positives, sample_weight, log_temp, logit_bias, loss_scale):
    tok_count, depth = tokens.shape[1:]
    features = proj_weight.shape[1]
    sketches = text_feats.shape[1]
    far, near, members = lax.axis_size("far"), lax.axis_size("near"), lax.axis_size("col")
    inv_count = 1.0 / (cycles * cycle_size * sketches)
    wide = features + LANES

    def in_hbm(*values):
        return [pltpu.with_memory_space_constraint(value, pltpu.HBM) for value in values]

    def in_vmem(*values):
        return [pltpu.with_memory_space_constraint(value, pltpu.VMEM) for value in values]

    def partner(block):
        return lax.ppermute(block, "near", [(i, (i + 1) % near) for i in range(near)])

    text_send = jnp.broadcast_to(text_feats, (far, sketches, features))
    near_texts = lax.all_to_all(text_send, "far", 0, 0, tiled=True)

    gain, weights = norm_gain.reshape(1, depth), proj_weight
    token_parts, weight_parts = 4, 1
    sketch_send, preact, pooled = pl.pallas_call(
        forward_kernel,
        out_shape=(
            pltpu.HBM((members, sketches, wide), BF16),
            pltpu.VMEM((tok_count, features), BF16),
            pltpu.VMEM((sketches, features), F32),
        ),
        in_specs=[HBM] * 6,
        out_specs=(HBM, VMEM, VMEM),
        scratch_shapes=[
            pltpu.VMEM((tok_count, depth), BF16),
            pltpu.VMEM((1, depth), F32),
            pltpu.VMEM((depth, features), BF16),
            pltpu.VMEM((1, 1, sketches), jnp.int32),
            pltpu.VMEM((1, sketches), jnp.int32),
            pltpu.VMEM((1, sketches), F32),
            pltpu.VMEM((tok_count, depth), BF16),
            pltpu.VMEM((sketches, wide), BF16),
            pltpu.SemaphoreType.DMA((4,)),
            pltpu.SemaphoreType.DMA((token_parts,)),
            pltpu.SemaphoreType.DMA((weight_parts,)),
            pltpu.SemaphoreType.DMA((members,)),
        ],
        compiler_params=params(),
        cost_estimate=pl.CostEstimate(flops=2 * tok_count * depth * features, bytes_accessed=5 << 20, transcendentals=tok_count * features),
        name="forward",
    )(*in_hbm(tokens, gain, weights, lengths, positives, sample_weight))
    sketch_all = lax.all_to_all(sketch_send, "col", 0, 0, tiled=True)
    other_texts = partner(near_texts)

    far_place, near_place, col = lax.axis_index("far"), lax.axis_index("near"), lax.axis_index("col")
    place = jnp.stack(
        [(f * members + col) * near + (near_place + h) % near for h in range(near) for f in range(far)]
    ).astype(jnp.int32)
    scalars = jnp.stack([log_temp, logit_bias, loss_scale])
    sketch_parts, near_part, other_part = pl.pallas_call(
        functools.partial(score_kernel, inv_count),
        out_shape=(
            pltpu.HBM((members, sketches, wide), BF16),
            pltpu.VMEM((far, sketches, features), F32),
            pltpu.VMEM((far, sketches, features), BF16),
        ),
        in_specs=[SMEM, SMEM, VMEM, VMEM, VMEM],
        out_specs=(HBM, VMEM, VMEM),
        scratch_shapes=[
            pltpu.VMEM((members, sketches, wide), BF16),
            pltpu.SemaphoreType.DMA((2,)),
        ],
        compiler_params=params(),
        name="score",
    )(scalars, place, *in_vmem(sketch_all, near_texts, other_texts))
    sketch_back = lax.all_to_all(sketch_parts, "col", 0, 0, tiled=True)
    text_sum = (near_part + partner(other_part).astype(F32)).astype(BF16)

    def lane_sums(parts):
        found = jnp.sum(parts[:, 0, features : features + 9].astype(F32), axis=0)
        return found[0:3] + (found[3:6] + found[6:9])

    def rounded(values):
        return lax.reduce_precision(values, 8, 7)

    row_sums = lane_sums(sketch_back)
    high = rounded(row_sums)
    middle = rounded(row_sums - high)
    row_lanes = jnp.pad(jnp.concatenate([high, middle, row_sums - high - middle]), (0, LANES - 9)).astype(BF16)
    text_parts = jnp.concatenate([text_sum, jnp.broadcast_to(row_lanes, (far, sketches, LANES))], axis=2)
    text_back = lax.all_to_all(text_parts, "far", 0, 0, tiled=True)

    grad_tokens = pl.pallas_call(
        backward_kernel,
        out_shape=pltpu.HBM(tokens.shape, BF16),
        in_specs=[VMEM] * 3 + [HBM] * 4,
        out_specs=HBM,
        scratch_shapes=[
            pltpu.VMEM((1, 1, sketches), jnp.int32),
            pltpu.VMEM((tok_count, depth), BF16),
            pltpu.VMEM((1, depth), F32),
            pltpu.VMEM((depth, features), BF16),
            pltpu.VMEM((tok_count, features), BF16),
            pltpu.VMEM((tok_count, depth), F32),
            pltpu.VMEM((tok_count, depth), BF16),
            pltpu.SemaphoreType.DMA((2,)),
            pltpu.SemaphoreType.DMA((token_parts,)),
            pltpu.SemaphoreType.DMA((weight_parts,)),
            pltpu.SemaphoreType.DMA((token_parts,)),
        ],
        compiler_params=params(),
        cost_estimate=pl.CostEstimate(flops=2 * tok_count * depth * features, bytes_accessed=5 << 20, transcendentals=0),
        name="backward",
    )(*in_vmem(pooled, preact, sketch_back), *in_hbm(lengths, tokens, gain, weights))
    sums_send = jnp.broadcast_to(jnp.pad(lane_sums(text_back), (0, LANES - 3)), (near * cycles, 8, LANES))
    sums_send, grad_tokens = lax.optimization_barrier((sums_send, grad_tokens))
    sums_all = lax.all_to_all(sums_send, ("near", "group"), 0, 0, tiled=True)
    sums = jnp.sum(sums_all[:, 0, :3], axis=0)

    grad_texts = pl.pallas_call(
        text_grad_kernel,
        out_shape=pltpu.HBM(text_feats.shape, F32),
        in_specs=[VMEM, HBM],
        out_specs=VMEM,
        scratch_shapes=[pltpu.VMEM((sketches, features), BF16), pltpu.SemaphoreType.DMA],
        name="text_grad",
    )(text_back, *in_hbm(text_feats))
    return (grad_tokens, grad_texts, sums[0], sums[1], sums[2])


def solution(mesh):
    cycle_size, cycles = mesh.shape["blk"], mesh.shape["group"]
    far, near = 4, 2
    tiles = jax.sharding.Mesh(
        mesh.devices.reshape(far, cycle_size // (far * near), near, cycles), ("far", "col", "near", "group")
    )
    blk = ("far", "col", "near")
    placed = (
        P("group", blk, None),
        P(),
        P(),
        P("group", blk, None),
        P("group", blk, None),
        P("group", blk),
        P("group", blk),
        P(),
        P(),
        P(),
    )
    return jax.shard_map(
        functools.partial(on_device, cycle_size, cycles),
        mesh=tiles,
        in_specs=placed,
        out_specs=(P("group", blk, None), P("group", blk, None), P(), P(), P()),
        check_vma=False,
    )
```

```python
import functools

import jax
import jax.numpy as jnp
from jax import lax
from jax.experimental import pallas as pl
from jax.experimental.pallas import tpu as pltpu
from jax.sharding import PartitionSpec as P

EPSILON = 1e-06
GELU_SCALE = 0.7978845608028654
GELU_CUBE = 0.044715
LANES = 128
VMEM_LIMIT = 32 * 1024 * 1024
F32 = jnp.float32
BF16 = jnp.bfloat16

VMEM = pl.BlockSpec(memory_space=pltpu.VMEM)
SMEM = pl.BlockSpec(memory_space=pltpu.SMEM)
HBM = pl.BlockSpec(memory_space=pltpu.HBM)


def params():
    return pltpu.CompilerParams(vmem_limit_bytes=VMEM_LIMIT)


def three_parts(values):
    high = values.astype(BF16).astype(F32)
    rest = values - high
    middle = rest.astype(BF16).astype(F32)
    return high, middle, rest - middle


def rows_to_column(row, count):
    here = lax.broadcasted_iota(jnp.int32, (count, count), 0)
    there = lax.broadcasted_iota(jnp.int32, (count, count), 1)
    return jnp.sum(jnp.where(here == there, row, 0.0), axis=1, keepdims=True)


def forward_kernel(
    tokens_hbm,
    gain_hbm,
    weight_hbm,
    lengths_hbm,
    positives_hbm,
    sample_hbm,
    send_hbm,
    preact_ref,
    pooled_ref,
    tokens_ref,
    gain_ref,
    weight_ref,
    lengths_ref,
    positives_ref,
    sample_ref,
    normed_ref,
    own_ref,
    small_sems,
    token_sems,
    weight_sems,
    send_sems,
):
    sketches = lengths_ref.shape[-1]
    tok_count, depth = tokens_ref.shape
    features = weight_ref.shape[1]
    token_parts, weight_parts = token_sems.shape[0], weight_sems.shape[0]
    block, width = tok_count // token_parts, features // weight_parts

    small = [
        pltpu.make_async_copy(source, target, small_sems.at[i])
        for i, (source, target) in enumerate(
            (
                (gain_hbm, gain_ref),
                (lengths_hbm, lengths_ref),
                (positives_hbm, positives_ref),
                (sample_hbm, sample_ref),
            )
        )
    ]
    token_copies = [
        pltpu.make_async_copy(
            tokens_hbm.at[0, pl.ds(i * block, block)], tokens_ref.at[pl.ds(i * block, block)], token_sems.at[i]
        )
        for i in range(token_parts)
    ]
    weight_copies = [
        pltpu.make_async_copy(
            weight_hbm.at[:, pl.ds(i * width, width)], weight_ref.at[:, pl.ds(i * width, width)], weight_sems.at[i]
        )
        for i in range(weight_parts)
    ]
    small[0].start()
    for copy in token_copies:
        copy.start()
    for copy in small[1:]:
        copy.start()
    for copy in weight_copies:
        copy.start()

    small[0].wait()
    gain = gain_ref[...]
    for i, copy in enumerate(token_copies):
        copy.wait()
        rows = pl.ds(i * block, block)
        inputs = tokens_ref[rows].astype(F32)
        inv_rms = lax.rsqrt(jnp.mean(inputs * inputs, axis=-1, keepdims=True) + EPSILON)
        normed_ref[rows] = (inputs * inv_rms * gain).astype(BF16)

    for copy in small[1:]:
        copy.wait()
    lens_row = lengths_ref[0].astype(F32)
    lens_col = rows_to_column(lens_row, sketches)
    here = lax.broadcasted_iota(jnp.int32, (sketches, sketches), 0)
    there = lax.broadcasted_iota(jnp.int32, (sketches, sketches), 1)
    ends = jnp.sum(jnp.where(there <= here, lens_row, 0.0), axis=1, keepdims=True)
    place = lax.broadcasted_iota(jnp.int32, (sketches, tok_count), 1).astype(F32)
    membership = jnp.where((place < ends) & (place >= ends - lens_col), 1.0, 0.0).astype(BF16)

    for i, copy in enumerate(weight_copies):
        copy.wait()
        columns = pl.ds(i * width, width)
        values = jnp.dot(normed_ref[...], weight_ref[:, columns], preferred_element_type=F32)
        square = values * values
        tanh_part = jnp.tanh(values * (GELU_SCALE + (GELU_SCALE * GELU_CUBE) * square))
        activated = (values * (0.5 + 0.5 * tanh_part)).astype(BF16)
        preact_ref[:, columns] = values.astype(BF16)
        pooled_ref[:, columns] = jnp.dot(membership, activated, preferred_element_type=F32) / lens_col

    pooled = pooled_ref[...]
    rnorm = lax.rsqrt(jnp.sum(pooled * pooled, axis=-1, keepdims=True) + EPSILON)
    embed = (pooled * rnorm).astype(BF16)
    paired = rows_to_column(positives_ref[...].astype(F32), sketches)
    paired_high = jnp.floor(paired * (1.0 / 16.0))
    weight = three_parts(rows_to_column(sample_ref[...], sketches))
    lane = lax.broadcasted_iota(jnp.int32, (sketches, LANES), 1)
    extra = jnp.zeros((sketches, LANES), F32)
    for i, column in enumerate((paired_high, paired - 16.0 * paired_high) + weight):
        extra = jnp.where(lane == i, column, extra)
    own_ref[:, :features] = embed
    own_ref[:, features:] = extra.astype(BF16)
    send_copies = [
        pltpu.make_async_copy(own_ref, send_hbm.at[i], send_sems.at[i]) for i in range(send_hbm.shape[0])
    ]
    for copy in send_copies:
        copy.start()
    for copy in send_copies:
        copy.wait()


def score_kernel(
    inv_count,
    scalars_ref,
    place_ref,
    sketch_ref,
    near_ref,
    other_ref,
    back_hbm,
    near_out_ref,
    other_out_ref,
    back_ref,
    out_sems,
):
    members, sketches = sketch_ref.shape[:2]
    far, _, features = near_ref.shape
    halves = 2
    rows, half = members * sketches, far * sketches
    texts = halves * half
    temper = jnp.exp(jnp.full((1, 1), scalars_ref[0], F32))
    column = lax.broadcasted_iota(jnp.int32, (1, texts), 1)
    first = jnp.zeros((1, texts), jnp.int32)
    for i in range(halves * far):
        first = jnp.where(column >= i * sketches, (place_ref[i] - i) * sketches, first)
    column = (column + first).astype(F32)
    text_in = jnp.concatenate(
        [ref[...].reshape(half, features) for ref in (near_ref, other_ref)], axis=0
    ).astype(F32)
    text_rnorm = lax.rsqrt(jnp.sum(text_in * text_in, axis=-1, keepdims=True) + EPSILON)
    text = (text_in * text_rnorm).astype(BF16)
    sketch = sketch_ref[:, :, :features].reshape(rows, features)
    extra = sketch_ref[:, :, features:].reshape(rows, LANES).astype(F32)
    paired = extra[:, 0:1] * 16.0 + extra[:, 1:2]
    weight = ((extra[:, 2:3] + extra[:, 3:4]) + extra[:, 4:5]) * inv_count
    dots = lax.dot_general(sketch, text, (((1,), (1,)), ((), ())), preferred_element_type=F32)
    logits = temper * dots + scalars_ref[1]
    is_pair = paired == column
    signs = jnp.where(is_pair, 1.0, -1.0)
    against = jnp.where(is_pair, -logits, logits)
    decay = jnp.exp(-jnp.abs(against))
    chance = jnp.where(against >= 0.0, 1.0, decay) / (1.0 + decay)
    coeffs = -weight * signs * chance
    scaled = (coeffs * (temper * scalars_ref[2])).astype(BF16)
    sketch_part = jnp.dot(scaled, text, preferred_element_type=F32).astype(BF16)
    back_ref[:, :, :features] = sketch_part.reshape(members, sketches, features)
    main = (slice(None), slice(None), pl.ds(0, features))
    lanes = (slice(None), slice(None), pl.ds(features, LANES))
    main_copy = pltpu.make_async_copy(back_ref.at[main], back_hbm.at[main], out_sems.at[0])
    main_copy.start()
    pair_loss = jnp.maximum(against, 0.0) + jnp.log1p(decay)

    def total(values):
        return jnp.sum(jnp.sum(values, axis=1, keepdims=True), axis=0, keepdims=True)

    lane = lax.broadcasted_iota(jnp.int32, (sketches, LANES), 1)
    sums = jnp.zeros((sketches, LANES), F32)
    for i, value in enumerate((total(weight * pair_loss), total(coeffs * temper * dots), total(coeffs))):
        for j, piece in enumerate(three_parts(value)):
            sums = jnp.where(lane == 3 * j + i, piece, sums)
    sums = sums.astype(BF16)
    for member in range(members):
        back_ref[member, :, features:] = sums
    lanes_copy = pltpu.make_async_copy(back_ref.at[lanes], back_hbm.at[lanes], out_sems.at[1])
    lanes_copy.start()
    text_part = lax.dot_general(scaled, sketch, (((0,), (0,)), ((), ())), preferred_element_type=F32)
    near_out_ref[...] = text_part[:half].reshape(far, sketches, features)
    other_out_ref[...] = text_part[half:].astype(BF16).reshape(far, sketches, features)
    main_copy.wait()
    lanes_copy.wait()


def backward_kernel(
    pooled_ref,
    preact_ref,
    parts_ref,
    lengths_hbm,
    tokens_hbm,
    gain_hbm,
    weight_hbm,
    out_hbm,
    lengths_ref,
    tokens_ref,
    gain_ref,
    weight_ref,
    act_ref,
    back_ref,
    out_ref,
    small_sems,
    token_sems,
    weight_sems,
    out_sems,
):
    sketches = lengths_ref.shape[-1]
    tok_count, depth = tokens_ref.shape
    features = preact_ref.shape[1]
    token_parts, weight_parts = token_sems.shape[0], weight_sems.shape[0]
    block, width = tok_count // token_parts, depth // weight_parts

    def rows(i):
        return pl.ds(i * block, block)

    def columns(i):
        return pl.ds(i * width, width)

    small = [
        pltpu.make_async_copy(lengths_hbm, lengths_ref, small_sems.at[0]),
        pltpu.make_async_copy(gain_hbm, gain_ref, small_sems.at[1]),
    ]
    weight_copies = [
        pltpu.make_async_copy(weight_hbm.at[columns(i)], weight_ref.at[columns(i)], weight_sems.at[i])
        for i in range(weight_parts)
    ]
    token_copies = [
        pltpu.make_async_copy(tokens_hbm.at[0, rows(i)], tokens_ref.at[rows(i)], token_sems.at[i])
        for i in range(token_parts)
    ]
    for copy in small + weight_copies + token_copies:
        copy.start()

    sketch_grad = jnp.sum(parts_ref[:, :, :features].astype(F32), axis=0)
    pooled = pooled_ref[...]
    rnorm = lax.rsqrt(jnp.sum(pooled * pooled, axis=-1, keepdims=True) + EPSILON)
    unit = pooled * rnorm
    along = jnp.sum(unit * sketch_grad, axis=-1, keepdims=True)
    for copy in small:
        copy.wait()
    lens_row = lengths_ref[0].astype(F32)
    lens_col = rows_to_column(lens_row, sketches)
    pool_grad = rnorm * (sketch_grad - unit * along) / lens_col
    high = pool_grad.astype(BF16)
    both = jnp.concatenate([high, (pool_grad - high.astype(F32)).astype(BF16)], axis=0)

    here = lax.broadcasted_iota(jnp.int32, (sketches, sketches), 0)
    there = lax.broadcasted_iota(jnp.int32, (sketches, sketches), 1)
    ends = jnp.sum(jnp.where(here <= there, lens_col, 0.0), axis=0, keepdims=True)
    place = lax.broadcasted_iota(jnp.int32, (tok_count, sketches), 0).astype(F32)
    membership = jnp.where((place < ends) & (place >= ends - lens_row), 1.0, 0.0).astype(BF16)
    membership = jnp.concatenate([membership, membership], axis=1)
    for i in range(token_parts):
        per_token = jnp.dot(membership[i * block : (i + 1) * block], both, preferred_element_type=F32)
        values = preact_ref[rows(i)].astype(F32)
        square = values * values
        tanh_part = jnp.tanh(values * (GELU_SCALE + (GELU_SCALE * GELU_CUBE) * square))
        slope = (0.5 + 0.5 * tanh_part) + values * (1.0 - tanh_part * tanh_part) * (
            0.5 * GELU_SCALE + (1.5 * GELU_SCALE * GELU_CUBE) * square
        )
        act_ref[rows(i)] = (per_token * slope).astype(BF16)

    for copy in token_copies:
        copy.wait()
    along_x = jnp.zeros((tok_count, 1), F32)
    power = jnp.zeros((tok_count, 1), F32)
    for i, copy in enumerate(weight_copies):
        copy.wait()
        grad = lax.dot_general(
            act_ref[...], weight_ref[columns(i)], (((1,), (1,)), ((), ())), preferred_element_type=F32
        )
        gain_part = grad * gain_ref[:, columns(i)]
        inputs = tokens_ref[:, columns(i)].astype(F32)
        back_ref[:, columns(i)] = gain_part
        along_x += jnp.sum(gain_part * inputs, axis=-1, keepdims=True)
        power += jnp.sum(inputs * inputs, axis=-1, keepdims=True)
    inv_rms = lax.rsqrt(power * (1.0 / depth) + EPSILON)
    shrink = inv_rms * inv_rms * inv_rms * (along_x * (1.0 / depth))
    out_copies = []
    for i in range(token_parts):
        span = slice(i * block, (i + 1) * block)
        inputs = tokens_ref[rows(i)].astype(F32)
        out_ref[rows(i)] = (inv_rms[span] * back_ref[rows(i)] - shrink[span] * inputs).astype(BF16)
        copy = pltpu.make_async_copy(out_ref.at[rows(i)], out_hbm.at[0, rows(i)], out_sems.at[i])
        copy.start()
        out_copies.append(copy)
    for copy in out_copies:
        copy.wait()


def text_grad_kernel(parts_ref, text_hbm, out_ref, text_ref, text_sem):
    copy = pltpu.make_async_copy(text_hbm.at[0], text_ref, text_sem)
    copy.start()
    text_grad = jnp.sum(parts_ref[:, :, : text_ref.shape[1]].astype(F32), axis=0)
    copy.wait()
    text_in = text_ref[...].astype(F32)
    rnorm = lax.rsqrt(jnp.sum(text_in * text_in, axis=-1, keepdims=True) + EPSILON)
    unit = text_in * rnorm
    along = jnp.sum(unit * text_grad, axis=-1, keepdims=True)
    out_ref[0] = rnorm * (text_grad - unit * along)


def on_device(cycle_size, cycles, tokens, norm_gain, proj_weight, text_feats, lengths, positives, sample_weight, log_temp, logit_bias, loss_scale):
    tok_count, depth = tokens.shape[1:]
    features = proj_weight.shape[1]
    sketches = text_feats.shape[1]
    far, near, members = lax.axis_size("far"), lax.axis_size("near"), lax.axis_size("col")
    inv_count = 1.0 / (cycles * cycle_size * sketches)
    wide = features + LANES

    def in_hbm(*values):
        return [pltpu.with_memory_space_constraint(value, pltpu.HBM) for value in values]

    def in_vmem(*values):
        return [pltpu.with_memory_space_constraint(value, pltpu.VMEM) for value in values]

    def partner(block):
        return lax.ppermute(block, "near", [(i, (i + 1) % near) for i in range(near)])

    text_send = jnp.broadcast_to(text_feats, (far, sketches, features))
    near_texts = lax.all_to_all(text_send, "far", 0, 0, tiled=True)

    gain, weights = norm_gain.reshape(1, depth), proj_weight
    token_parts, weight_parts = 4, 1
    sketch_send, preact, pooled = pl.pallas_call(
        forward_kernel,
        out_shape=(
            pltpu.HBM((members, sketches, wide), BF16),
            pltpu.VMEM((tok_count, features), BF16),
            pltpu.VMEM((sketches, features), F32),
        ),
        in_specs=[HBM] * 6,
        out_specs=(HBM, VMEM, VMEM),
        scratch_shapes=[
            pltpu.VMEM((tok_count, depth), BF16),
            pltpu.VMEM((1, depth), F32),
            pltpu.VMEM((depth, features), BF16),
            pltpu.VMEM((1, 1, sketches), jnp.int32),
            pltpu.VMEM((1, sketches), jnp.int32),
            pltpu.VMEM((1, sketches), F32),
            pltpu.VMEM((tok_count, depth), BF16),
            pltpu.VMEM((sketches, wide), BF16),
            pltpu.SemaphoreType.DMA((4,)),
            pltpu.SemaphoreType.DMA((token_parts,)),
            pltpu.SemaphoreType.DMA((weight_parts,)),
            pltpu.SemaphoreType.DMA((members,)),
        ],
        compiler_params=params(),
        cost_estimate=pl.CostEstimate(flops=2 * tok_count * depth * features, bytes_accessed=5 << 20, transcendentals=tok_count * features),
        name="forward",
    )(*in_hbm(tokens, gain, weights, lengths, positives, sample_weight))
    sketch_all = lax.all_to_all(sketch_send, "col", 0, 0, tiled=True)
    other_texts = partner(near_texts)

    far_place, near_place, col = lax.axis_index("far"), lax.axis_index("near"), lax.axis_index("col")
    place = jnp.stack(
        [(f * members + col) * near + (near_place + h) % near for h in range(near) for f in range(far)]
    ).astype(jnp.int32)
    scalars = jnp.stack([log_temp, logit_bias, loss_scale])
    sketch_parts, near_part, other_part = pl.pallas_call(
        functools.partial(score_kernel, inv_count),
        out_shape=(
            pltpu.HBM((members, sketches, wide), BF16),
            pltpu.VMEM((far, sketches, features), F32),
            pltpu.VMEM((far, sketches, features), BF16),
        ),
        in_specs=[SMEM, SMEM, VMEM, VMEM, VMEM],
        out_specs=(HBM, VMEM, VMEM),
        scratch_shapes=[
            pltpu.VMEM((members, sketches, wide), BF16),
            pltpu.SemaphoreType.DMA((2,)),
        ],
        compiler_params=params(),
        name="score",
    )(scalars, place, *in_vmem(sketch_all, near_texts, other_texts))
    sketch_back = lax.all_to_all(sketch_parts, "col", 0, 0, tiled=True)
    text_sum = (near_part + partner(other_part).astype(F32)).astype(BF16)

    def lane_sums(parts):
        found = jnp.sum(parts[:, 0, features : features + 9].astype(F32), axis=0)
        return found[0:3] + (found[3:6] + found[6:9])

    def rounded(values):
        return lax.reduce_precision(values, 8, 7)

    row_sums = lane_sums(sketch_back)
    high = rounded(row_sums)
    middle = rounded(row_sums - high)
    row_lanes = jnp.pad(jnp.concatenate([high, middle, row_sums - high - middle]), (0, LANES - 9)).astype(BF16)
    text_parts = jnp.concatenate([text_sum, jnp.broadcast_to(row_lanes, (far, sketches, LANES))], axis=2)
    text_back = lax.all_to_all(text_parts, "far", 0, 0, tiled=True)

    grad_tokens = pl.pallas_call(
        backward_kernel,
        out_shape=pltpu.HBM(tokens.shape, BF16),
        in_specs=[VMEM] * 3 + [HBM] * 4,
        out_specs=HBM,
        scratch_shapes=[
            pltpu.VMEM((1, 1, sketches), jnp.int32),
            pltpu.VMEM((tok_count, depth), BF16),
            pltpu.VMEM((1, depth), F32),
            pltpu.VMEM((depth, features), BF16),
            pltpu.VMEM((tok_count, features), BF16),
            pltpu.VMEM((tok_count, depth), F32),
            pltpu.VMEM((tok_count, depth), BF16),
            pltpu.SemaphoreType.DMA((2,)),
            pltpu.SemaphoreType.DMA((token_parts,)),
            pltpu.SemaphoreType.DMA((weight_parts,)),
            pltpu.SemaphoreType.DMA((token_parts,)),
        ],
        compiler_params=params(),
        cost_estimate=pl.CostEstimate(flops=2 * tok_count * depth * features, bytes_accessed=5 << 20, transcendentals=0),
        name="backward",
    )(*in_vmem(pooled, preact, sketch_back), *in_hbm(lengths, tokens, gain, weights))
    sums_send = jnp.broadcast_to(jnp.pad(lane_sums(text_back), (0, LANES - 3)), (near * cycles, 1, LANES))
    sums_send, grad_tokens = lax.optimization_barrier((sums_send, grad_tokens))
    sums_all = lax.all_to_all(sums_send, ("near", "group"), 0, 0, tiled=True)
    sums = jnp.sum(sums_all[:, 0, :3], axis=0)

    grad_texts = pl.pallas_call(
        text_grad_kernel,
        out_shape=pltpu.HBM(text_feats.shape, F32),
        in_specs=[VMEM, HBM],
        out_specs=VMEM,
        scratch_shapes=[pltpu.VMEM((sketches, features), BF16), pltpu.SemaphoreType.DMA],
        name="text_grad",
    )(text_back, *in_hbm(text_feats))
    return (grad_tokens, grad_texts, sums[0], sums[1], sums[2])


def solution(mesh):
    cycle_size, cycles = mesh.shape["blk"], mesh.shape["group"]
    far, near = 4, 2
    tiles = jax.sharding.Mesh(
        mesh.devices.reshape(far, cycle_size // (far * near), near, cycles), ("far", "col", "near", "group")
    )
    blk = ("far", "col", "near")
    placed = (
        P("group", blk, None),
        P(),
        P(),
        P("group", blk, None),
        P("group", blk, None),
        P("group", blk),
        P("group", blk),
        P(),
        P(),
        P(),
    )
    return jax.shard_map(
        functools.partial(on_device, cycle_size, cycles),
        mesh=tiles,
        in_specs=placed,
        out_specs=(P("group", blk, None), P("group", blk, None), P(), P(), P()),
        check_vma=False,
    )
```

```python
import functools

import jax
import jax.numpy as jnp
from jax import lax
from jax.experimental import pallas as pl
from jax.experimental.pallas import tpu as pltpu
from jax.sharding import PartitionSpec as P

EPSILON = 1e-06
GELU_SCALE = 0.7978845608028654
GELU_CUBE = 0.044715
LANES = 128
VMEM_LIMIT = 32 * 1024 * 1024
F32 = jnp.float32
BF16 = jnp.bfloat16

VMEM = pl.BlockSpec(memory_space=pltpu.VMEM)
SMEM = pl.BlockSpec(memory_space=pltpu.SMEM)
HBM = pl.BlockSpec(memory_space=pltpu.HBM)


def params():
    return pltpu.CompilerParams(vmem_limit_bytes=VMEM_LIMIT)


def three_parts(values):
    high = values.astype(BF16).astype(F32)
    rest = values - high
    middle = rest.astype(BF16).astype(F32)
    return high, middle, rest - middle


def rows_to_column(row, count):
    here = lax.broadcasted_iota(jnp.int32, (count, count), 0)
    there = lax.broadcasted_iota(jnp.int32, (count, count), 1)
    return jnp.sum(jnp.where(here == there, row, 0.0), axis=1, keepdims=True)


def forward_kernel(
    tokens_hbm,
    gain_hbm,
    weight_hbm,
    lengths_hbm,
    positives_hbm,
    sample_hbm,
    send_hbm,
    preact_ref,
    pooled_ref,
    tokens_ref,
    gain_ref,
    weight_ref,
    lengths_ref,
    positives_ref,
    sample_ref,
    normed_ref,
    own_ref,
    small_sems,
    token_sems,
    weight_sems,
    send_sems,
):
    sketches = lengths_ref.shape[-1]
    tok_count, depth = tokens_ref.shape
    features = weight_ref.shape[1]
    token_parts, weight_parts = token_sems.shape[0], weight_sems.shape[0]
    block, width = tok_count // token_parts, features // weight_parts

    small = [
        pltpu.make_async_copy(source, target, small_sems.at[i])
        for i, (source, target) in enumerate(
            (
                (gain_hbm, gain_ref),
                (lengths_hbm, lengths_ref),
                (positives_hbm, positives_ref),
                (sample_hbm, sample_ref),
            )
        )
    ]
    token_copies = [
        pltpu.make_async_copy(
            tokens_hbm.at[0, pl.ds(i * block, block)], tokens_ref.at[pl.ds(i * block, block)], token_sems.at[i]
        )
        for i in range(token_parts)
    ]
    weight_copies = [
        pltpu.make_async_copy(
            weight_hbm.at[:, pl.ds(i * width, width)], weight_ref.at[:, pl.ds(i * width, width)], weight_sems.at[i]
        )
        for i in range(weight_parts)
    ]
    small[0].start()
    for copy in token_copies:
        copy.start()
    for copy in small[1:]:
        copy.start()
    for copy in weight_copies:
        copy.start()

    small[0].wait()
    gain = gain_ref[...]
    for i, copy in enumerate(token_copies):
        copy.wait()
        rows = pl.ds(i * block, block)
        inputs = tokens_ref[rows].astype(F32)
        inv_rms = lax.rsqrt(jnp.mean(inputs * inputs, axis=-1, keepdims=True) + EPSILON)
        normed_ref[rows] = (inputs * inv_rms * gain).astype(BF16)

    for copy in small[1:]:
        copy.wait()
    lens_row = lengths_ref[0].astype(F32)
    lens_col = rows_to_column(lens_row, sketches)
    here = lax.broadcasted_iota(jnp.int32, (sketches, sketches), 0)
    there = lax.broadcasted_iota(jnp.int32, (sketches, sketches), 1)
    ends = jnp.sum(jnp.where(there <= here, lens_row, 0.0), axis=1, keepdims=True)
    place = lax.broadcasted_iota(jnp.int32, (sketches, tok_count), 1).astype(F32)
    membership = jnp.where((place < ends) & (place >= ends - lens_col), 1.0, 0.0).astype(BF16)

    for i, copy in enumerate(weight_copies):
        copy.wait()
        columns = pl.ds(i * width, width)
        values = jnp.dot(normed_ref[...], weight_ref[:, columns], preferred_element_type=F32)
        square = values * values
        tanh_part = jnp.tanh(values * (GELU_SCALE + (GELU_SCALE * GELU_CUBE) * square))
        activated = (values * (0.5 + 0.5 * tanh_part)).astype(BF16)
        preact_ref[:, columns] = values.astype(BF16)
        pooled_ref[:, columns] = jnp.dot(membership, activated, preferred_element_type=F32) / lens_col

    pooled = pooled_ref[...]
    rnorm = lax.rsqrt(jnp.sum(pooled * pooled, axis=-1, keepdims=True) + EPSILON)
    embed = (pooled * rnorm).astype(BF16)
    paired = rows_to_column(positives_ref[...].astype(F32), sketches)
    paired_high = jnp.floor(paired * (1.0 / 16.0))
    weight = three_parts(rows_to_column(sample_ref[...], sketches))
    lane = lax.broadcasted_iota(jnp.int32, (sketches, LANES), 1)
    extra = jnp.zeros((sketches, LANES), F32)
    for i, column in enumerate((paired_high, paired - 16.0 * paired_high) + weight):
        extra = jnp.where(lane == i, column, extra)
    own_ref[:, :features] = embed
    own_ref[:, features:] = extra.astype(BF16)
    send_copies = [
        pltpu.make_async_copy(own_ref, send_hbm.at[i], send_sems.at[i]) for i in range(send_hbm.shape[0])
    ]
    for copy in send_copies:
        copy.start()
    for copy in send_copies:
        copy.wait()


def score_kernel(
    inv_count,
    scalars_ref,
    place_ref,
    sketch_ref,
    near_ref,
    other_ref,
    back_hbm,
    near_out_ref,
    other_out_ref,
    back_ref,
    out_sems,
):
    members, sketches = sketch_ref.shape[:2]
    far, _, features = near_ref.shape
    halves = 2
    rows, half = members * sketches, far * sketches
    texts = halves * half
    temper = jnp.exp(jnp.full((1, 1), scalars_ref[0], F32))
    column = lax.broadcasted_iota(jnp.int32, (1, texts), 1)
    first = jnp.zeros((1, texts), jnp.int32)
    for i in range(halves * far):
        first = jnp.where(column >= i * sketches, (place_ref[i] - i) * sketches, first)
    column = (column + first).astype(F32)
    text_in = other_ref[...].reshape(half, features).astype(F32)
    text_rnorm = lax.rsqrt(jnp.sum(text_in * text_in, axis=-1, keepdims=True) + EPSILON)
    text = jnp.concatenate([near_ref[...].reshape(half, features), (text_in * text_rnorm).astype(BF16)], axis=0)
    sketch = sketch_ref[:, :, :features].reshape(rows, features)
    extra = sketch_ref[:, :, features:].reshape(rows, LANES).astype(F32)
    paired = extra[:, 0:1] * 16.0 + extra[:, 1:2]
    weight = ((extra[:, 2:3] + extra[:, 3:4]) + extra[:, 4:5]) * inv_count
    dots = lax.dot_general(sketch, text, (((1,), (1,)), ((), ())), preferred_element_type=F32)
    logits = temper * dots + scalars_ref[1]
    is_pair = paired == column
    signs = jnp.where(is_pair, 1.0, -1.0)
    against = jnp.where(is_pair, -logits, logits)
    decay = jnp.exp(-jnp.abs(against))
    chance = jnp.where(against >= 0.0, 1.0, decay) / (1.0 + decay)
    coeffs = -weight * signs * chance
    scaled = (coeffs * (temper * scalars_ref[2])).astype(BF16)
    sketch_part = jnp.dot(scaled, text, preferred_element_type=F32).astype(BF16)
    back_ref[:, :, :features] = sketch_part.reshape(members, sketches, features)
    main = (slice(None), slice(None), pl.ds(0, features))
    lanes = (slice(None), slice(None), pl.ds(features, LANES))
    main_copy = pltpu.make_async_copy(back_ref.at[main], back_hbm.at[main], out_sems.at[0])
    main_copy.start()
    pair_loss = jnp.maximum(against, 0.0) + jnp.log1p(decay)

    def total(values):
        return jnp.sum(jnp.sum(values, axis=1, keepdims=True), axis=0, keepdims=True)

    lane = lax.broadcasted_iota(jnp.int32, (sketches, LANES), 1)
    sums = jnp.zeros((sketches, LANES), F32)
    for i, value in enumerate((total(weight * pair_loss), total(coeffs * temper * dots), total(coeffs))):
        for j, piece in enumerate(three_parts(value)):
            sums = jnp.where(lane == 3 * j + i, piece, sums)
    sums = sums.astype(BF16)
    for member in range(members):
        back_ref[member, :, features:] = sums
    lanes_copy = pltpu.make_async_copy(back_ref.at[lanes], back_hbm.at[lanes], out_sems.at[1])
    lanes_copy.start()
    text_part = lax.dot_general(scaled, sketch, (((0,), (0,)), ((), ())), preferred_element_type=F32)
    near_out_ref[...] = text_part[:half].reshape(far, sketches, features)
    other_out_ref[...] = text_part[half:].astype(BF16).reshape(far, sketches, features)
    main_copy.wait()
    lanes_copy.wait()


def backward_kernel(
    pooled_ref,
    preact_ref,
    parts_ref,
    lengths_hbm,
    tokens_hbm,
    gain_hbm,
    weight_hbm,
    out_hbm,
    lengths_ref,
    tokens_ref,
    gain_ref,
    weight_ref,
    act_ref,
    back_ref,
    out_ref,
    small_sems,
    token_sems,
    weight_sems,
    out_sems,
):
    sketches = lengths_ref.shape[-1]
    tok_count, depth = tokens_ref.shape
    features = preact_ref.shape[1]
    token_parts, weight_parts = token_sems.shape[0], weight_sems.shape[0]
    block, width = tok_count // token_parts, depth // weight_parts

    def rows(i):
        return pl.ds(i * block, block)

    def columns(i):
        return pl.ds(i * width, width)

    small = [
        pltpu.make_async_copy(lengths_hbm, lengths_ref, small_sems.at[0]),
        pltpu.make_async_copy(gain_hbm, gain_ref, small_sems.at[1]),
    ]
    weight_copies = [
        pltpu.make_async_copy(weight_hbm.at[columns(i)], weight_ref.at[columns(i)], weight_sems.at[i])
        for i in range(weight_parts)
    ]
    token_copies = [
        pltpu.make_async_copy(tokens_hbm.at[0, rows(i)], tokens_ref.at[rows(i)], token_sems.at[i])
        for i in range(token_parts)
    ]
    for copy in small + weight_copies + token_copies:
        copy.start()

    sketch_grad = jnp.sum(parts_ref[:, :, :features].astype(F32), axis=0)
    pooled = pooled_ref[...]
    rnorm = lax.rsqrt(jnp.sum(pooled * pooled, axis=-1, keepdims=True) + EPSILON)
    unit = pooled * rnorm
    along = jnp.sum(unit * sketch_grad, axis=-1, keepdims=True)
    for copy in small:
        copy.wait()
    lens_row = lengths_ref[0].astype(F32)
    lens_col = rows_to_column(lens_row, sketches)
    pool_grad = rnorm * (sketch_grad - unit * along) / lens_col
    high = pool_grad.astype(BF16)
    both = jnp.concatenate([high, (pool_grad - high.astype(F32)).astype(BF16)], axis=0)

    here = lax.broadcasted_iota(jnp.int32, (sketches, sketches), 0)
    there = lax.broadcasted_iota(jnp.int32, (sketches, sketches), 1)
    ends = jnp.sum(jnp.where(here <= there, lens_col, 0.0), axis=0, keepdims=True)
    place = lax.broadcasted_iota(jnp.int32, (tok_count, sketches), 0).astype(F32)
    membership = jnp.where((place < ends) & (place >= ends - lens_row), 1.0, 0.0).astype(BF16)
    membership = jnp.concatenate([membership, membership], axis=1)
    for i in range(token_parts):
        per_token = jnp.dot(membership[i * block : (i + 1) * block], both, preferred_element_type=F32)
        values = preact_ref[rows(i)].astype(F32)
        square = values * values
        tanh_part = jnp.tanh(values * (GELU_SCALE + (GELU_SCALE * GELU_CUBE) * square))
        slope = (0.5 + 0.5 * tanh_part) + values * (1.0 - tanh_part * tanh_part) * (
            0.5 * GELU_SCALE + (1.5 * GELU_SCALE * GELU_CUBE) * square
        )
        act_ref[rows(i)] = (per_token * slope).astype(BF16)

    for copy in token_copies:
        copy.wait()
    along_x = jnp.zeros((tok_count, 1), F32)
    power = jnp.zeros((tok_count, 1), F32)
    for i, copy in enumerate(weight_copies):
        copy.wait()
        grad = lax.dot_general(
            act_ref[...], weight_ref[columns(i)], (((1,), (1,)), ((), ())), preferred_element_type=F32
        )
        gain_part = grad * gain_ref[:, columns(i)]
        inputs = tokens_ref[:, columns(i)].astype(F32)
        back_ref[:, columns(i)] = gain_part
        along_x += jnp.sum(gain_part * inputs, axis=-1, keepdims=True)
        power += jnp.sum(inputs * inputs, axis=-1, keepdims=True)
    inv_rms = lax.rsqrt(power * (1.0 / depth) + EPSILON)
    shrink = inv_rms * inv_rms * inv_rms * (along_x * (1.0 / depth))
    out_copies = []
    for i in range(token_parts):
        span = slice(i * block, (i + 1) * block)
        inputs = tokens_ref[rows(i)].astype(F32)
        out_ref[rows(i)] = (inv_rms[span] * back_ref[rows(i)] - shrink[span] * inputs).astype(BF16)
        copy = pltpu.make_async_copy(out_ref.at[rows(i)], out_hbm.at[0, rows(i)], out_sems.at[i])
        copy.start()
        out_copies.append(copy)
    for copy in out_copies:
        copy.wait()


def text_grad_kernel(parts_ref, text_hbm, out_ref, text_ref, text_sem):
    copy = pltpu.make_async_copy(text_hbm.at[0], text_ref, text_sem)
    copy.start()
    text_grad = jnp.sum(parts_ref[:, :, : text_ref.shape[1]].astype(F32), axis=0)
    copy.wait()
    text_in = text_ref[...].astype(F32)
    rnorm = lax.rsqrt(jnp.sum(text_in * text_in, axis=-1, keepdims=True) + EPSILON)
    unit = text_in * rnorm
    along = jnp.sum(unit * text_grad, axis=-1, keepdims=True)
    out_ref[0] = rnorm * (text_grad - unit * along)


def on_device(cycle_size, cycles, tokens, norm_gain, proj_weight, text_feats, lengths, positives, sample_weight, log_temp, logit_bias, loss_scale):
    tok_count, depth = tokens.shape[1:]
    features = proj_weight.shape[1]
    sketches = text_feats.shape[1]
    far, near, members = lax.axis_size("far"), lax.axis_size("near"), lax.axis_size("col")
    inv_count = 1.0 / (cycles * cycle_size * sketches)
    wide = features + LANES

    def in_hbm(*values):
        return [pltpu.with_memory_space_constraint(value, pltpu.HBM) for value in values]

    def in_vmem(*values):
        return [pltpu.with_memory_space_constraint(value, pltpu.VMEM) for value in values]

    def partner(block):
        return lax.ppermute(block, "near", [(i, (i + 1) % near) for i in range(near)])

    text_send = jnp.broadcast_to(text_feats, (far, sketches, features))
    near_texts = lax.all_to_all(text_send, "far", 0, 0, tiled=True)

    gain, weights = norm_gain.reshape(1, depth), proj_weight
    token_parts, weight_parts = 4, 1
    sketch_send, preact, pooled = pl.pallas_call(
        forward_kernel,
        out_shape=(
            pltpu.HBM((members, sketches, wide), BF16),
            pltpu.VMEM((tok_count, features), BF16),
            pltpu.VMEM((sketches, features), F32),
        ),
        in_specs=[HBM] * 6,
        out_specs=(HBM, VMEM, VMEM),
        scratch_shapes=[
            pltpu.VMEM((tok_count, depth), BF16),
            pltpu.VMEM((1, depth), F32),
            pltpu.VMEM((depth, features), BF16),
            pltpu.VMEM((1, 1, sketches), jnp.int32),
            pltpu.VMEM((1, sketches), jnp.int32),
            pltpu.VMEM((1, sketches), F32),
            pltpu.VMEM((tok_count, depth), BF16),
            pltpu.VMEM((sketches, wide), BF16),
            pltpu.SemaphoreType.DMA((4,)),
            pltpu.SemaphoreType.DMA((token_parts,)),
            pltpu.SemaphoreType.DMA((weight_parts,)),
            pltpu.SemaphoreType.DMA((members,)),
        ],
        compiler_params=params(),
        cost_estimate=pl.CostEstimate(flops=2 * tok_count * depth * features, bytes_accessed=5 << 20, transcendentals=tok_count * features),
        name="forward",
    )(*in_hbm(tokens, gain, weights, lengths, positives, sample_weight))
    sketch_all = lax.all_to_all(sketch_send, "col", 0, 0, tiled=True)
    other_texts = partner(near_texts)
    near_in = near_texts.astype(F32)
    near_embed = (near_in * lax.rsqrt(jnp.sum(near_in * near_in, axis=-1, keepdims=True) + EPSILON)).astype(BF16)

    far_place, near_place, col = lax.axis_index("far"), lax.axis_index("near"), lax.axis_index("col")
    place = jnp.stack(
        [(f * members + col) * near + (near_place + h) % near for h in range(near) for f in range(far)]
    ).astype(jnp.int32)
    scalars = jnp.stack([log_temp, logit_bias, loss_scale])
    sketch_parts, near_part, other_part = pl.pallas_call(
        functools.partial(score_kernel, inv_count),
        out_shape=(
            pltpu.HBM((members, sketches, wide), BF16),
            pltpu.VMEM((far, sketches, features), F32),
            pltpu.VMEM((far, sketches, features), BF16),
        ),
        in_specs=[SMEM, SMEM, VMEM, VMEM, VMEM],
        out_specs=(HBM, VMEM, VMEM),
        scratch_shapes=[
            pltpu.VMEM((members, sketches, wide), BF16),
            pltpu.SemaphoreType.DMA((2,)),
        ],
        compiler_params=params(),
        name="score",
    )(scalars, place, *in_vmem(sketch_all, near_embed, other_texts))
    sketch_back = lax.all_to_all(sketch_parts, "col", 0, 0, tiled=True)
    text_sum = (near_part + partner(other_part).astype(F32)).astype(BF16)

    def lane_sums(parts):
        found = jnp.sum(parts[:, 0, features : features + 9].astype(F32), axis=0)
        return found[0:3] + (found[3:6] + found[6:9])

    def rounded(values):
        return lax.reduce_precision(values, 8, 7)

    row_sums = lane_sums(sketch_back)
    high = rounded(row_sums)
    middle = rounded(row_sums - high)
    row_lanes = jnp.pad(jnp.concatenate([high, middle, row_sums - high - middle]), (0, LANES - 9)).astype(BF16)
    text_parts = jnp.concatenate([text_sum, jnp.broadcast_to(row_lanes, (far, sketches, LANES))], axis=2)
    text_back = lax.all_to_all(text_parts, "far", 0, 0, tiled=True)

    grad_tokens = pl.pallas_call(
        backward_kernel,
        out_shape=pltpu.HBM(tokens.shape, BF16),
        in_specs=[VMEM] * 3 + [HBM] * 4,
        out_specs=HBM,
        scratch_shapes=[
            pltpu.VMEM((1, 1, sketches), jnp.int32),
            pltpu.VMEM((tok_count, depth), BF16),
            pltpu.VMEM((1, depth), F32),
            pltpu.VMEM((depth, features), BF16),
            pltpu.VMEM((tok_count, features), BF16),
            pltpu.VMEM((tok_count, depth), F32),
            pltpu.VMEM((tok_count, depth), BF16),
            pltpu.SemaphoreType.DMA((2,)),
            pltpu.SemaphoreType.DMA((token_parts,)),
            pltpu.SemaphoreType.DMA((weight_parts,)),
            pltpu.SemaphoreType.DMA((token_parts,)),
        ],
        compiler_params=params(),
        cost_estimate=pl.CostEstimate(flops=2 * tok_count * depth * features, bytes_accessed=5 << 20, transcendentals=0),
        name="backward",
    )(*in_vmem(pooled, preact, sketch_back), *in_hbm(lengths, tokens, gain, weights))
    sums_send = jnp.broadcast_to(jnp.pad(lane_sums(text_back), (0, LANES - 3)), (near * cycles, 1, LANES))
    sums_send, grad_tokens = lax.optimization_barrier((sums_send, grad_tokens))
    sums_all = lax.all_to_all(sums_send, ("near", "group"), 0, 0, tiled=True)
    sums = jnp.sum(sums_all[:, 0, :3], axis=0)

    grad_texts = pl.pallas_call(
        text_grad_kernel,
        out_shape=pltpu.HBM(text_feats.shape, F32),
        in_specs=[VMEM, HBM],
        out_specs=VMEM,
        scratch_shapes=[pltpu.VMEM((sketches, features), BF16), pltpu.SemaphoreType.DMA],
        name="text_grad",
    )(text_back, *in_hbm(text_feats))
    return (grad_tokens, grad_texts, sums[0], sums[1], sums[2])


def solution(mesh):
    cycle_size, cycles = mesh.shape["blk"], mesh.shape["group"]
    far, near = 4, 2
    tiles = jax.sharding.Mesh(
        mesh.devices.reshape(far, cycle_size // (far * near), near, cycles), ("far", "col", "near", "group")
    )
    blk = ("far", "col", "near")
    placed = (
        P("group", blk, None),
        P(),
        P(),
        P("group", blk, None),
        P("group", blk, None),
        P("group", blk),
        P("group", blk),
        P(),
        P(),
        P(),
    )
    return jax.shard_map(
        functools.partial(on_device, cycle_size, cycles),
        mesh=tiles,
        in_specs=placed,
        out_specs=(P("group", blk, None), P("group", blk, None), P(), P(), P()),
        check_vma=False,
    )
```
